512 devices in a mesh: space: 64 (over y, z), chan: 8 (over x, core).
Axes of the slice: x: 4, y: 8, z: 8, core: 2. Of those that a mesh axis runs over, the one named last changes fastest.
Arguments:
- state_field: bfloat16 [384, 192, 1440], P('chan', 'space'), may hold values from -6 to 6
- slot_wave: int32 [1152], replicated, may hold values from 0 to 720, as said below
- spectral_filter: bfloat16 [1152, 2, 384, 720], P('space', None, 'chan'), may hold values from -4 to 4
- kan_coef: bfloat16 [6, 384, 384], P(None, 'chan'), may hold values from -0.125 to 0.125
Outputs:
- mixed_out: bfloat16 [384, 192, 1440], P('chan', 'space')
The draws below stay inside these ranges and needn't reach their ends.
Inputs may be any that keep to these rules, and one draw needn't show every extreme that they name: `slot_wave`: each wavenumber 0 to 719 is held by exactly one slot, every other slot holds 720; owner d holds slots d * 18 to (d+1) * 18 - 1, and some owner has all its slots filled.
All inputs are finite; a program needn't handle non-finite values.
Results may differ from the reference program's by a relative error of at most 0.025.
Values may be sent and summed in bfloat16 or wider, within the bound.
A program may use at most 128 MiB of HBM per device.

```python
import math
import jax
import jax.numpy as jnp
from jax import lax

C = 384
NLON = 1440
MMAX = 720
LMAX = 720
BASIS = 6
LAT = 192
MSLOT = 18
N_SPACE = 64
N_CHAN = 8


def draw_slot_wave(key, part):
    key = jax.random.fold_in(key, 11)
    slot_total = N_SPACE * MSLOT
    owner_key, score_key, wave_key = jax.random.split(key, 3)
    full_owner = jax.random.randint(owner_key, (), 0, N_SPACE)
    scores = jax.random.permutation(score_key, slot_total).astype(jnp.int32)
    slot_index = jnp.arange(slot_total, dtype=jnp.int32)
    owner = slot_index // MSLOT
    scores = jnp.where(owner == full_owner, slot_index - slot_total, scores)
    ordering = jnp.argsort(scores, stable=True)
    ranking = jnp.argsort(ordering, stable=True).astype(jnp.int32)
    wave_ids = jax.random.permutation(wave_key, MMAX).astype(jnp.int32)
    picked = jnp.take(wave_ids, jnp.minimum(ranking, MMAX - 1))
    return jnp.where(ranking < MMAX, picked, MMAX).astype(jnp.int32)


def block_levels(stream_key, extent, cuts, smallest, high):
    loudness, own = 1.0, jax.random.fold_in(stream_key, 6)
    for axis_at, parts in cuts:
        draws = jnp.exp(jax.random.uniform(jax.random.fold_in(own, axis_at), (parts,), jnp.float32, smallest / len(cuts), high / len(cuts)))
        loudness = loudness * jnp.repeat(draws, extent[axis_at] // parts).reshape([-1 if axis == axis_at else 1 for axis in range(len(extent))])
    return loudness


def scatter_about(rng, dims, spread, reach, cuts=(), held_as=jnp.bfloat16):
    level = block_levels(rng, dims, cuts, -0.22, 0.18) if cuts else 1.0
    entries = jax.random.normal(rng, dims, jnp.float32) * spread * level
    return jnp.minimum(jnp.maximum(entries, -reach), reach).astype(held_as)


def setup_inputs(seed: int = 0) -> dict:
    arg_keys = jax.random.split(jax.random.key(seed), 5)
    state_field = scatter_about(arg_keys[0], (C, LAT, NLON), 1.0, 6.0, ((0, 8), (1, 64)))
    slot_wave = draw_slot_wave(jax.random.fold_in(arg_keys[4], 71), 0)
    spectral_filter = scatter_about(arg_keys[2], (N_SPACE * MSLOT, 2, C, LMAX), 1.0, 4.0, ((0, 64), (2, 8)))
    kan_coef = scatter_about(arg_keys[3], (BASIS, C, C), (BASIS * C) ** -0.5, 0.125, ((1, 8),))
    return {"state_field": state_field, "slot_wave": slot_wave, "spectral_filter": spectral_filter, "kan_coef": kan_coef}


def zonal_tables(nlon, wave_total):
    wave_order = jnp.arange(wave_total, dtype=jnp.int32)
    points = jnp.arange(nlon, dtype=jnp.int32)
    phases = wave_order[:, None] * points[None, :] % nlon
    angles = phases.astype(jnp.float32) * (2.0 * math.pi / nlon)
    cosine = jnp.cos(angles)
    sine_part = jnp.sin(angles)
    forward = jnp.stack([cosine, -sine_part], axis=1).reshape(2 * wave_total, nlon) / nlon
    factor = jnp.where(wave_order == 0, 1.0, 2.0).astype(jnp.float32)[:, None]
    inverse = jnp.stack([factor * cosine, -factor * sine_part], axis=1).reshape(2 * wave_total, nlon)
    return (forward.astype(jnp.bfloat16), inverse.astype(jnp.bfloat16))

def band_grid(lat_all, lmax):
    row_index = jnp.arange(lat_all, dtype=jnp.int32).astype(jnp.float32)
    colatitude = 0.5 * math.pi + (row_index + 0.5 - 0.5 * lat_all) * (math.pi / lmax)
    weights = 2.0 * math.pi * math.pi / lmax * jnp.sin(colatitude)
    return (colatitude, weights)

def legendre_table(wave_ids, colatitude, lmax):
    cosine = jnp.cos(colatitude)[None, :]
    wave_order = wave_ids.astype(jnp.float32)[:, None]
    log_first = 0.5 * (jnp.log((2.0 * wave_order + 1.0) / (4.0 * math.pi)) + lax.lgamma(wave_order + 0.5) - lax.lgamma(wave_order + 1.0) - 0.5 * math.log(math.pi))
    first_value = jnp.exp(log_first + wave_order * jnp.log(jnp.sin(colatitude))[None, :])
    per_block = 1
    for candidate in (24, 20, 16, 12, 10, 8, 6, 4, 2):
        if lmax % candidate == 0 and per_block == 1:
            per_block = candidate

    def advance(state_pair, block_index):
        before, earlier = state_pair
        collected = []
        for offset in range(per_block):
            degree = (block_index * per_block + offset).astype(jnp.float32)
            prior_degree = degree - 1.0
            rising = jnp.sqrt((4.0 * degree * degree - 1.0) / jnp.maximum(degree * degree - wave_order * wave_order, 1.0))
            falling = jnp.sqrt(jnp.maximum(prior_degree * prior_degree - wave_order * wave_order, 0.0) / (4.0 * prior_degree * prior_degree - 1.0))
            general = rising * (cosine * before - falling * earlier)
            second = cosine * jnp.sqrt(2.0 * wave_order + 3.0) * before
            current = jnp.where(degree < wave_order, 0.0, jnp.where(degree == wave_order, first_value, jnp.where(degree == wave_order + 1.0, second, general)))
            earlier = before
            before = current
            collected.append(current)
        return ((before, earlier), jnp.stack(collected))
    zero_state = jnp.zeros((wave_ids.shape[0], colatitude.shape[0]), jnp.float32)
    _, stacked = lax.scan(advance, (zero_state, zero_state), jnp.arange(lmax // per_block, dtype=jnp.int32))
    return stacked.reshape(lmax, wave_ids.shape[0], colatitude.shape[0])

def filter_modes(spectrum, filter_gain):
    count = spectrum.shape[0]
    shaped = spectrum.reshape(count, 2, filter_gain.shape[2], filter_gain.shape[3])
    real_part = shaped[:, 0]
    imag_part = shaped[:, 1]
    gain_real = filter_gain[:, 0]
    gain_imag = filter_gain[:, 1]
    result = jnp.stack([gain_real * real_part - gain_imag * imag_part, gain_real * imag_part + gain_imag * real_part], axis=1)
    return result.reshape(spectrum.shape).astype(jnp.bfloat16)

def expand_basis(activity):
    upcast = activity.astype(jnp.float32)
    squashed = jnp.tanh(upcast)
    constant = jnp.ones_like(squashed)
    quadratic = 2.0 * squashed * squashed - 1.0
    cubic_term = 2.0 * squashed * quadratic - squashed
    quartic = 2.0 * squashed * cubic_term - quadratic
    base_branch = upcast * jax.nn.sigmoid(upcast)
    return jnp.stack([base_branch, constant, squashed, quadratic, cubic_term, quartic]).astype(jnp.bfloat16)

def reference(state_field, slot_wave, spectral_filter, kan_coef):
    lat_all = state_field.shape[1]
    forward, inverse = zonal_tables(NLON, MMAX)
    zonal_coeff = lax.dot_general(forward, state_field, (((1,), (2,)), ((), ())), preferred_element_type=jnp.float32).astype(jnp.bfloat16)
    colatitude, weights = band_grid(lat_all, LMAX)
    slot_total = slot_wave.shape[0]
    matches = (slot_wave[None, :] == jnp.arange(MMAX, dtype=jnp.int32)[:, None]).astype(jnp.int32)
    position = lax.optimization_barrier(jnp.sum(matches * jnp.arange(slot_total, dtype=jnp.int32)[None, :], axis=1)).astype(jnp.int32)
    block_size = 8
    blocks = MMAX // block_size
    zonal_blocks = zonal_coeff.reshape(blocks, block_size, 2 * C, lat_all)

    def spectral(inputs):
        block_index, coefficients = inputs
        wave_ids = (block_index * block_size + jnp.arange(block_size, dtype=jnp.int32)).astype(jnp.int32)
        legendre = legendre_table(wave_ids, colatitude, LMAX)
        analysis = (legendre * weights[None, None, :]).astype(jnp.bfloat16)
        synthesis = legendre.astype(jnp.bfloat16)
        spectrum = jnp.einsum('kqj,lkj->kql', coefficients.astype(jnp.float32), analysis.astype(jnp.float32), precision=lax.Precision.HIGHEST)
        filter_gain = jnp.take(spectral_filter, jnp.take(position, wave_ids), axis=0).astype(jnp.float32)
        filtered = filter_modes(spectrum, filter_gain)
        rebuilt = jnp.einsum('kql,lkj->kqj', filtered.astype(jnp.float32), synthesis.astype(jnp.float32), precision=lax.Precision.HIGHEST)
        return rebuilt.astype(jnp.bfloat16)
    synthesized = lax.map(spectral, (jnp.arange(blocks, dtype=jnp.int32), zonal_blocks))
    synthesized = synthesized.reshape(2 * MMAX, C, lat_all)
    spatial = lax.dot_general(synthesized, inverse, (((0,), (0,)), ((), ())), preferred_element_type=jnp.float32)
    updated = (state_field.astype(jnp.float32) + spatial).astype(jnp.bfloat16)
    groups = N_CHAN
    group_width = C // groups
    row_count = lat_all * NLON
    flat_input = updated.reshape(groups, group_width, row_count)
    coef_groups = jnp.transpose(kan_coef.reshape(BASIS, groups, group_width, C), (1, 0, 2, 3))

    def accumulate(running, inputs):
        channel_piece, coef_piece = inputs
        basis_rows = expand_basis(channel_piece).reshape(BASIS * group_width, row_count)
        partial_value = lax.dot_general(coef_piece.reshape(BASIS * group_width, C), basis_rows, (((0,), (0,)), ((), ())), preferred_element_type=jnp.float32)
        rounded = lax.optimization_barrier(partial_value.astype(jnp.bfloat16))
        return (running + rounded.astype(jnp.float32), 0)
    running, _ = lax.scan(accumulate, jnp.zeros((C, row_count), jnp.float32), (flat_input, coef_groups))
    return running.astype(jnp.bfloat16).reshape(C, lat_all, NLON)
```

```python
import math

import jax
import jax.numpy as jnp
import ml_dtypes
import numpy as np
from jax import lax
from jax.experimental import pallas as pl
from jax.experimental.pallas import tpu as pltpu
from jax.sharding import PartitionSpec as P

NLON = 1440
MMAX = 720
LMAX = 720
BASIS = 6
MPAD = 768
NPAD = 1536
SLOTS = 18
MAIN = 16
SPACES = 64
CHANS = 8
CDEV = 48
LDEV = 3
LAT = 192
ROWS = 48
COLS = 1408
PART = 640
DEG_SLOTS = 24
F32 = jnp.float32
BF16 = jnp.bfloat16

VMEM = pl.BlockSpec(memory_space=pltpu.VMEM)
SMEM = pl.BlockSpec(memory_space=pltpu.SMEM)
PARAMS = pltpu.CompilerParams(vmem_limit_bytes=56 * 1024 * 1024)


def make_tables():
    m = np.arange(MMAX)[:, None]
    n = np.arange(NLON)[None, :]
    angle = (m * n % NLON) * (2.0 * np.pi / NLON)
    cos, sin = np.cos(angle), np.sin(angle)
    forward = np.zeros((NLON, 2 * MPAD))
    forward[:, :MMAX] = cos.T / NLON
    forward[:, MPAD : MPAD + MMAX] = -sin.T / NLON
    factor = np.where(m == 0, 1.0, 2.0)
    inverse = np.zeros((2 * MPAD, NPAD))
    inverse[:MMAX, :NLON] = factor * cos
    inverse[MPAD : MPAD + MMAX, :NLON] = -factor * sin
    lat = np.arange(LAT)
    colat = 0.5 * np.pi + (lat + 0.5 - 0.5 * LAT) * (np.pi / LMAX)
    weights = (2.0 * np.pi * np.pi / LMAX * np.sin(colat)).astype(np.float32)
    order = (3 * np.arange(SPACES)[None, :] + np.arange(LDEV)[:, None]).reshape(-1)
    xrow = np.zeros((8, 256), np.float32)
    xrow[:, :LAT] = np.cos(colat)[order]
    first = np.zeros((MMAX + 8, 256), np.float32)
    for wave in range(MMAX):
        base = 0.5 * (
            math.log((2.0 * wave + 1.0) / (4.0 * math.pi))
            + math.lgamma(wave + 0.5)
            - math.lgamma(wave + 1.0)
            - 0.5 * math.log(math.pi)
        )
        first[wave, :LAT] = np.exp(base + wave * np.log(np.sin(colat)))[order]
    degree = np.arange(LMAX, dtype=np.float64)
    root = np.sqrt(np.maximum(4.0 * degree * degree - 1.0, 1.0))
    steps = np.stack([degree * degree, root, 1.0 / root]).astype(np.float32)
    return (
        forward.astype(ml_dtypes.bfloat16),
        inverse.astype(ml_dtypes.bfloat16),
        weights,
        xrow,
        first,
        steps,
    )


def one_hot(cols_row, start, size):
    waves = lax.broadcasted_iota(jnp.int32, (MPAD, size), 0)
    return jnp.where(waves == cols_row[0:1, start : start + size], 1.0, 0.0).astype(BF16)


def third_of(pair, shape):
    lane = lax.broadcasted_iota(jnp.int32, shape, 1)
    return jnp.where(lane >= 64, (2 * pair + 1) % 3, (2 * pair) % 3)


def pack_kernel(x_ref, table_ref, cols_ref, weight_ref, out_ref, zonal, packed, rows):
    here = lax.axis_index("space")
    for lat in range(LDEV):
        weight = weight_ref[here * LDEV + lat]
        for k in range(2):
            part = jnp.dot(
                x_ref[lat], table_ref[:, k * MPAD : (k + 1) * MPAD], preferred_element_type=F32
            )
            at = lat * 96 + k * CDEV
            zonal[at : at + CDEV, :] = (part * weight).astype(BF16)
    cols = cols_ref[...]
    coeff = zonal[...]
    for start in range(0, COLS, 128):
        packed[:, start : start + 128] = jnp.dot(
            coeff, one_hot(cols, start, 128), preferred_element_type=F32
        )
    for pair in range(MAIN // 2):
        for lat in range(LDEV):
            at = lat * 96
            main = packed[at : at + 96, pair * 128 : pair * 128 + 128]
            extra = jnp.zeros((32, 128), F32)
            if pair < 3:
                wide = packed[at : at + 96, 1024 + pair * 128 : 1024 + pair * 128 + 128]
                third = third_of(pair, (32, 128))
                for th in range(3):
                    extra = jnp.where(third == th, wide[th * 32 : th * 32 + 32], extra)
            turned = jnp.concatenate([main, extra], axis=0).T
            for half in range(2):
                at_row = lat * 16 + pair * 2 + half
                rows[pl.ds(at_row, 64, stride=ROWS), :] = turned[half * 64 : half * 64 + 64]
    out_ref[...] = rows[...].astype(BF16)


def legendre_kernel(wave_ref, steps_ref, x_ref, first_ref, out_ref, grown, order_ref, start_ref):
    base = lax.axis_index("space") * SLOTS
    for slot in range(DEG_SLOTS):
        wave = wave_ref[base + slot] if slot < SLOTS else MMAX
        order_ref[slot : slot + 1, :] = jnp.full((1, 128), wave, jnp.int32)
        start_ref[slot : slot + 1, :] = first_ref[pl.ds(wave, 1), :]
    order = order_ref[...]
    square = order.astype(F32) * order.astype(F32)
    first_a, first_b = start_ref[:, 0:128], start_ref[:, 128:256]
    x_a = jnp.broadcast_to(x_ref[0:1, 0:128], (DEG_SLOTS, 128))
    x_b = jnp.broadcast_to(x_ref[0:1, 128:256], (DEG_SLOTS, 128))

    def advance(block, carry):
        now_a, before_a, now_b, before_b, falling = carry
        for offset in range(8):
            degree = block * 8 + offset
            gap = steps_ref[0, degree] - square
            inverse_root = lax.rsqrt(jnp.maximum(gap, 1.0))
            rising = steps_ref[1, degree] * inverse_root
            starts = order == degree
            next_a = jnp.where(starts, first_a, rising * (x_a * now_a - falling * before_a))
            next_b = jnp.where(starts, first_b, rising * (x_b * now_b - falling * before_b))
            falling = gap * inverse_root * steps_ref[2, degree]
            now_a, before_a, now_b, before_b = next_a, now_a, next_b, now_b
            grown[0, pl.ds(degree * DEG_SLOTS, DEG_SLOTS), :] = next_a
            grown[1, pl.ds(degree * DEG_SLOTS, DEG_SLOTS), :] = next_b
        return now_a, before_a, now_b, before_b, falling

    zero = jnp.zeros((DEG_SLOTS, 128), F32)
    lax.fori_loop(0, LMAX // 8, advance, (zero, zero, zero, zero, zero))

    def spread(slot, carry):
        for half in range(2):
            out_ref[slot, :, half * 128 : half * 128 + 128] = grown[
                half, pl.ds(slot, LMAX, stride=DEG_SLOTS), :
            ].astype(BF16)
        return carry

    lax.fori_loop(0, SLOTS, spread, 0)


def spectral_kernel(rows_ref, table_ref, gain_ref, out_ref, rows, spread, made):
    rows[...] = rows_ref[...].astype(F32)
    for row in range(MAIN):
        stack = jnp.concatenate(
            [rows[pl.ds(lat * 16 + row, 64, stride=ROWS), :] for lat in range(LDEV)]
            + [jnp.zeros((64, 128), F32)],
            axis=0,
        )
        turned = stack.T.astype(BF16)
        spread[row] = turned[0:96]
        if row < 6:
            at = 32 * (row % 3)
            spread[MAIN + row // 3, at : at + 32, :] = turned[96:128]

    def one(slot, carry):
        table = table_ref[slot]
        spectrum = lax.dot_general(
            spread[slot], table, (((1,), (1,)), ((), ())), preferred_element_type=F32
        )
        real, imag = spectrum[0:CDEV], spectrum[CDEV:96]
        gain_real = gain_ref[slot, 0].astype(F32)
        gain_imag = gain_ref[slot, 1].astype(F32)
        filtered = jnp.concatenate(
            [gain_real * real - gain_imag * imag, gain_real * imag + gain_imag * real], axis=0
        ).astype(BF16)
        made[slot] = jnp.dot(filtered, table, preferred_element_type=F32)
        return carry

    lax.fori_loop(0, SLOTS, one, 0)
    for row in range(MAIN):
        extra = jnp.zeros((32, 256), F32)
        if row < 6:
            at = 32 * (row % 3)
            extra = made[MAIN + row // 3, at : at + 32, :]
        turned = jnp.concatenate([made[row], extra], axis=0).T
        for lat in range(LDEV):
            rows[pl.ds(lat * 16 + row, 64, stride=ROWS), :] = turned[lat * 64 : lat * 64 + 64]
    out_ref[...] = rows[...].astype(BF16)


def inverse_kernel(rows_ref, table_ref, cols_ref, x_ref, out_ref, rows, gathered, modes):
    rows[...] = rows_ref[...].astype(F32)
    for pair in range(MAIN // 2):
        for lat in range(LDEV):
            at = lat * 96
            turned = (
                jnp.concatenate(
                    [
                        rows[pl.ds(lat * 16 + pair * 2 + half, 64, stride=ROWS), :]
                        for half in range(2)
                    ],
                    axis=0,
                )
            ).T
            gathered[at : at + 96, pair * 128 : pair * 128 + 128] = turned[0:96].astype(BF16)
            if pair < 3:
                third = third_of(pair, (32, 128))
                for th in range(3):
                    gathered[
                        at + th * 32 : at + th * 32 + 32,
                        1024 + pair * 128 : 1024 + pair * 128 + 128,
                    ] = jnp.where(third == th, turned[96:128], 0.0).astype(BF16)
    cols = cols_ref[...]
    total = jnp.zeros((288, MPAD), F32)
    for start in range(0, COLS, 128):
        total += lax.dot_general(
            gathered[:, start : start + 128],
            one_hot(cols, start, 128),
            (((1,), (1,)), ((), ())),
            preferred_element_type=F32,
        )
    for lat in range(LDEV):
        for k in range(2):
            at = lat * 96 + k * CDEV
            modes[lat * CDEV : lat * CDEV + CDEV, k * MPAD : (k + 1) * MPAD] = total[
                at : at + CDEV
            ].astype(BF16)
    for block in range(12):
        lanes = slice(block * 128, block * 128 + 128)
        spatial = jnp.dot(modes[...], table_ref[:, lanes], preferred_element_type=F32)
        chip, inner = block // 3, block % 3
        for lat in range(LDEV):
            if block < 11:
                old = x_ref[lat, :, lanes].astype(F32)
            else:
                old = jnp.concatenate(
                    [x_ref[lat, :, 1408:1440], jnp.zeros((CDEV, 96), BF16)], axis=1
                ).astype(F32)
            new = (old + spatial[lat * CDEV : lat * CDEV + CDEV]).astype(BF16)
            if lat == 0:
                places = [(2 * chip, inner)]
            elif lat == 2:
                places = [(2 * chip + 1, inner)]
            elif inner < 2:
                places = [(2 * chip, 3 + inner)]
            else:
                places = [(2 * chip + 1, 3), (2 * chip + 1, 4)]
            for part, at in places:
                out_ref[part, :, at * 128 : at * 128 + 128] = new


def coef_kernel(coef_ref, out_ref, bias_ref):
    for k in range(BASIS):
        turned = jnp.concatenate([coef_ref[g, k] for g in range(CHANS)], axis=0).astype(F32).T
        if k == 1:
            bias_ref[...] = jnp.broadcast_to(
                jnp.sum(turned, axis=1, keepdims=True), bias_ref.shape
            )
        else:
            at = (k if k == 0 else k - 1) * 384
            out_ref[:, at : at + 384] = turned.astype(BF16)


def mixer_kernel(u_ref, coef_ref, bias_ref, out_ref):
    for block in range(5):
        lanes = slice(block * 128, block * 128 + 128)
        u = u_ref[:, lanes].astype(F32)
        t = jnp.tanh(u)
        base = 0.5 * u * (1.0 + jnp.tanh(0.5 * u))
        second = 2.0 * t * t - 1.0
        third = 2.0 * t * second - t
        fourth = 2.0 * t * third - second
        basis = jnp.concatenate(
            [piece.astype(BF16) for piece in (base, t, second, third, fourth)], axis=0
        )
        mixed = jnp.dot(coef_ref[...], basis, preferred_element_type=F32)
        out_ref[:, lanes] = (mixed + bias_ref[...]).astype(BF16)


def shards(state_field, slot_wave, spectral_filter, kan_coef):
    forward, inverse, weights, xrow, first, steps = make_tables()
    x = jnp.transpose(state_field, (1, 0, 2))
    slots = slot_wave.reshape(SPACES, SLOTS)
    cols = jnp.concatenate(
        [slots[:, :MAIN].T.reshape(-1)] + [slots[:, 16]] * 3 + [slots[:, 17]] * 3
    )
    cols = jnp.broadcast_to(cols[None, :], (8, COLS))
    coef_all = lax.all_gather(kan_coef, "chan")
    packed = pl.pallas_call(
        pack_kernel,
        out_shape=jax.ShapeDtypeStruct((SPACES * ROWS, 128), BF16),
        in_specs=[VMEM, VMEM, VMEM, SMEM],
        out_specs=VMEM,
        scratch_shapes=[
            pltpu.VMEM((288, MPAD), BF16),
            pltpu.VMEM((288, COLS), F32),
            pltpu.VMEM((SPACES * ROWS, 128), F32),
        ],
        compiler_params=PARAMS,
    )(x, forward, cols, weights)
    arrived = lax.all_to_all(
        packed.reshape(SPACES, ROWS, 128), "space", split_axis=0, concat_axis=0
    ).reshape(SPACES * ROWS, 128)
    legendre = pl.pallas_call(
        legendre_kernel,
        out_shape=jax.ShapeDtypeStruct((SLOTS, LMAX, 256), BF16),
        in_specs=[SMEM, SMEM, VMEM, VMEM],
        out_specs=VMEM,
        scratch_shapes=[
            pltpu.VMEM((2, LMAX * DEG_SLOTS, 128), F32),
            pltpu.VMEM((DEG_SLOTS, 128), jnp.int32),
            pltpu.VMEM((DEG_SLOTS, 256), F32),
        ],
        compiler_params=PARAMS,
        cost_estimate=pl.CostEstimate(flops=400_000_000, bytes_accessed=8_000_000, transcendentals=0),
    )(slot_wave, steps, xrow, first)
    coef, bias = pl.pallas_call(
        coef_kernel,
        out_shape=(
            jax.ShapeDtypeStruct((384, 5 * 384), BF16),
            jax.ShapeDtypeStruct((384, 128), F32),
        ),
        in_specs=[VMEM],
        out_specs=(VMEM, VMEM),
        compiler_params=PARAMS,
    )(coef_all)
    rebuilt = pl.pallas_call(
        spectral_kernel,
        out_shape=jax.ShapeDtypeStruct((SPACES * ROWS, 128), BF16),
        in_specs=[VMEM, VMEM, VMEM],
        out_specs=VMEM,
        scratch_shapes=[
            pltpu.VMEM((SPACES * ROWS, 128), F32),
            pltpu.VMEM((SLOTS, 96, 256), BF16),
            pltpu.VMEM((SLOTS, 96, 256), F32),
        ],
        compiler_params=PARAMS,
    )(arrived, legendre, spectral_filter)
    returned = lax.all_to_all(
        rebuilt.reshape(SPACES, ROWS, 128), "space", split_axis=0, concat_axis=0
    ).reshape(SPACES * ROWS, 128)
    updated = pl.pallas_call(
        inverse_kernel,
        out_shape=jax.ShapeDtypeStruct((CHANS, CDEV, PART), BF16),
        in_specs=[VMEM, VMEM, VMEM, VMEM],
        out_specs=VMEM,
        scratch_shapes=[
            pltpu.VMEM((SPACES * ROWS, 128), F32),
            pltpu.VMEM((288, COLS), BF16),
            pltpu.VMEM((144, 2 * MPAD), BF16),
        ],
        compiler_params=PARAMS,
    )(returned, inverse, cols, x)
    whole = lax.all_to_all(updated, "chan", split_axis=0, concat_axis=0).reshape(384, PART)
    mixed = pl.pallas_call(
        mixer_kernel,
        out_shape=jax.ShapeDtypeStruct((384, PART), BF16),
        in_specs=[VMEM, VMEM, VMEM],
        out_specs=VMEM,
        compiler_params=PARAMS,
    )(whole, coef, bias)
    back = lax.all_to_all(mixed.reshape(CHANS, CDEV, PART), "chan", split_axis=0, concat_axis=0)
    lats = []
    for lat in range(LDEV):
        blocks = []
        for chip in range(4):
            if lat == 0:
                blocks.append(back[2 * chip, :, 0:384])
            elif lat == 2:
                blocks.append(back[2 * chip + 1, :, 0:384])
            else:
                blocks.append(back[2 * chip, :, 384:640])
                blocks.append(back[2 * chip + 1, :, 384:512])
        lats.append(jnp.concatenate(blocks, axis=1)[:, :NLON])
    return jnp.stack(lats, axis=1)


def solution(mesh):
    in_specs = (
        P("chan", "space", None),
        P(),
        P("space", None, "chan", None),
        P(None, "chan", None),
    )
    out_specs = P("chan", "space", None)
    return jax.shard_map(shards, mesh=mesh, in_specs=in_specs, out_specs=out_specs, check_vma=False)
```

```python
import math

import jax
import jax.numpy as jnp
import ml_dtypes
import numpy as np
from jax import lax
from jax.experimental import pallas as pl
from jax.experimental.pallas import tpu as pltpu
from jax.sharding import PartitionSpec as P

NLON = 1440
MMAX = 720
LMAX = 720
BASIS = 6
MPAD = 768
NPAD = 1536
SLOTS = 18
MAIN = 16
SPACES = 64
CHANS = 8
CDEV = 48
LDEV = 3
LAT = 192
ROWS = 48
COLS = 1408
PART = 640
DEG_SLOTS = 24
CHUNK = 240
F32 = jnp.float32
BF16 = jnp.bfloat16

VMEM = pl.BlockSpec(memory_space=pltpu.VMEM)
SMEM = pl.BlockSpec(memory_space=pltpu.SMEM)
HBM = pl.BlockSpec(memory_space=pl.ANY)
MESH = pl.DeviceIdType.MESH


def make_tables():
    m = np.arange(MMAX)[:, None]
    n = np.arange(NLON)[None, :]
    angle = (m * n % NLON) * (2.0 * np.pi / NLON)
    cos, sin = np.cos(angle), np.sin(angle)
    forward = np.zeros((2, NLON, MPAD))
    forward[0, :, :MMAX] = cos.T / NLON
    forward[1, :, :MMAX] = -sin.T / NLON
    factor = np.where(m == 0, 1.0, 2.0)
    inverse = np.zeros((2 * MPAD, NPAD))
    inverse[:MMAX, :NLON] = factor * cos
    inverse[MPAD : MPAD + MMAX, :NLON] = -factor * sin
    lat = np.arange(LAT)
    colat = 0.5 * np.pi + (lat + 0.5 - 0.5 * LAT) * (np.pi / LMAX)
    weights = (2.0 * np.pi * np.pi / LMAX * np.sin(colat)).astype(np.float32)
    order = (3 * np.arange(SPACES)[None, :] + np.arange(LDEV)[:, None]).reshape(-1)
    xrow = np.zeros((8, 256), np.float32)
    xrow[:, :LAT] = np.cos(colat)[order]
    first = np.zeros((MMAX + 8, 256), np.float32)
    for wave in range(MMAX):
        base = 0.5 * (
            math.log((2.0 * wave + 1.0) / (4.0 * math.pi))
            + math.lgamma(wave + 0.5)
            - math.lgamma(wave + 1.0)
            - 0.5 * math.log(math.pi)
        )
        first[wave, :LAT] = np.exp(base + wave * np.log(np.sin(colat)))[order]
    degree = np.arange(LMAX, dtype=np.float64)
    root = np.sqrt(np.maximum(4.0 * degree * degree - 1.0, 1.0))
    steps = np.stack([degree * degree, root, 1.0 / root]).astype(np.float32)
    return (
        forward.astype(ml_dtypes.bfloat16),
        inverse.astype(ml_dtypes.bfloat16),
        weights,
        xrow,
        first,
        steps,
    )


def one_hot(cols_row, start, size):
    waves = lax.broadcasted_iota(jnp.int32, (MPAD, size), 0)
    return jnp.where(waves == cols_row[0:1, start : start + size], 1.0, 0.0).astype(BF16)


def third_of(pair, shape):
    lane = lax.broadcasted_iota(jnp.int32, shape, 1)
    return jnp.where(lane >= 64, (2 * pair + 1) % 3, (2 * pair) % 3)


def far(i):
    return 4 + ((i + 1) // 2) * (1 - 2 * (i % 2))


def block_kernel(
    x_hbm,
    forward_hbm,
    inverse_hbm,
    gain_hbm,
    coef_hbm,
    wave_ref,
    weight_ref,
    steps_ref,
    cols_ref,
    xrow_ref,
    first_ref,
    out_ref,
    x_ref,
    forward_ref,
    inverse_ref,
    gain_ref,
    coefs,
    load_sem,
    send_sem,
    recv_sem,
    chan_send,
    chan_recv,
    hot,
    zonal,
    packed,
    rows,
    out_rows,
    in_rows,
    order_ref,
    start_ref,
    grown,
    legendre,
    spread,
    made,
    back_rows,
    got_rows,
    coef_ref,
    bias_ref,
    gathered,
    modes,
    updated,
    whole,
    mixed,
    final,
):
    here = lax.axis_index("space")
    group = lax.axis_index("chan")
    here_y, here_z = here // 8, here % 8

    def space_peer(k):
        return lax.rem(here_y + far(k // 8), 8) * 8 + lax.rem(here_z + far(k % 8), 8)

    loads = [
        pltpu.make_async_copy(source, target, load_sem.at[i])
        for i, (source, target) in enumerate(
            (
                (x_hbm, x_ref),
                (forward_hbm, forward_ref),
                (inverse_hbm, inverse_ref),
                (gain_hbm, gain_ref),
                (coef_hbm, coefs.at[group]),
            )
        )
    ]
    load_x, load_forward, load_inverse, load_gain, load_coef = loads
    for load in loads:
        load.start()

    barrier = pltpu.get_barrier_semaphore()

    def greet_space(k, carry):
        pl.semaphore_signal(
            barrier, inc=1, device_id={"space": space_peer(k)}, device_id_type=MESH
        )
        return carry

    def greet_chan(k, carry):
        pl.semaphore_signal(
            barrier, inc=1, device_id={"chan": lax.rem(group + k, CHANS)}, device_id_type=MESH
        )
        return carry

    lax.fori_loop(0, SPACES - 1, greet_space, 0)
    lax.fori_loop(1, CHANS, greet_chan, 0)

    def send_space(source, target, step, lat):
        def one(k, carry):
            peer = space_peer(k)
            pltpu.make_async_remote_copy(
                src_ref=source.at[lat, pl.ds(pl.multiple_of(peer * 16, 16), 16)],
                dst_ref=target.at[lat, pl.ds(pl.multiple_of(here * 16, 16), 16)],
                send_sem=send_sem.at[step, lat],
                recv_sem=recv_sem.at[step, lat],
                device_id={"space": peer},
                device_id_type=MESH,
            ).start()
            return carry

        lax.fori_loop(0, SPACES - 1, one, 0)
        own = pl.ds(pl.multiple_of(here * 16, 16), 16)
        target[lat, own, :] = source[lat, own, :]

    def wait_space(source, target, sem, step, lat):
        most = pl.ds(0, (SPACES - 1) * 16)
        pltpu.make_async_copy(
            source.at[lat, most], target.at[lat, most], sem.at[step, lat]
        ).wait()

    def send_chan(source, target, step):
        def one(k, carry):
            peer = lax.rem(group + far(k), CHANS)
            pltpu.make_async_remote_copy(
                src_ref=source.at[peer],
                dst_ref=target.at[group],
                send_sem=chan_send.at[step],
                recv_sem=chan_recv.at[step],
                device_id={"chan": peer},
                device_id_type=MESH,
            ).start()
            return carry

        lax.fori_loop(0, CHANS - 1, one, 0)
        target[group] = source[group]

    def wait_chan(source, target, sem, step):
        most = pl.ds(0, CHANS - 1)
        pltpu.make_async_copy(source.at[most], target.at[most], sem.at[step]).wait()

    cols = cols_ref[...]
    for start in range(0, COLS, 128):
        hot[:, start : start + 128] = one_hot(cols, start, 128)
    load_x.wait()
    load_forward.wait()
    for lat in range(LDEV):
        weight = weight_ref[here * LDEV + lat]
        for k in range(2):
            part = jnp.dot(x_ref[lat], forward_ref[k], preferred_element_type=F32)
            zonal[k * CDEV : k * CDEV + CDEV, :] = (part * weight).astype(BF16)
        packed[...] = jnp.dot(zonal[...], hot[...], preferred_element_type=F32)
        for pair in range(MAIN // 2):
            main = packed[:, pair * 128 : pair * 128 + 128]
            extra = jnp.zeros((32, 128), F32)
            if pair < 3:
                wide = packed[:, 1024 + pair * 128 : 1024 + pair * 128 + 128]
                third = third_of(pair, (32, 128))
                for th in range(3):
                    extra = jnp.where(third == th, wide[th * 32 : th * 32 + 32], extra)
            turned = jnp.concatenate([main, extra], axis=0).T
            for half in range(2):
                rows[lat, pl.ds(pair * 2 + half, 64, stride=16), :] = turned[
                    half * 64 : half * 64 + 64
                ]
        out_rows[lat] = rows[lat].astype(BF16)
        if lat == 0:
            pl.semaphore_wait(barrier, SPACES - 1 + CHANS - 1)
        send_space(out_rows, in_rows, 0, lat)

    load_coef.wait()

    def send_coef(k, carry):
        pltpu.make_async_remote_copy(
            src_ref=coefs.at[group],
            dst_ref=coefs.at[group],
            send_sem=chan_send.at[0],
            recv_sem=chan_recv.at[0],
            device_id={"chan": lax.rem(group + far(k), CHANS)},
            device_id_type=MESH,
        ).start()
        return carry

    lax.fori_loop(0, CHANS - 1, send_coef, 0)

    for slot in range(DEG_SLOTS):
        wave = wave_ref[here * SLOTS + slot] if slot < SLOTS else MMAX
        order_ref[slot : slot + 1, :] = jnp.full((1, 128), wave, jnp.int32)
        start_ref[slot : slot + 1, :] = first_ref[pl.ds(wave, 1), :]
    order = order_ref[...]
    square = order.astype(F32) * order.astype(F32)
    first_a, first_b = start_ref[:, 0:128], start_ref[:, 128:256]
    x_a = jnp.broadcast_to(xrow_ref[0:1, 0:128], (DEG_SLOTS, 128))
    x_b = jnp.broadcast_to(xrow_ref[0:1, 128:256], (DEG_SLOTS, 128))
    zero = jnp.zeros((DEG_SLOTS, 128), F32)
    state = (zero, zero, zero, zero, zero)
    for chunk in range(LMAX // CHUNK):

        def advance(block, carry, chunk=chunk):
            now_a, before_a, now_b, before_b, falling = carry
            for offset in range(8):
                at = block * 8 + offset
                degree = chunk * CHUNK + at
                gap = steps_ref[0, degree] - square
                inverse_root = lax.rsqrt(jnp.maximum(gap, 1.0))
                rising = steps_ref[1, degree] * inverse_root
                starts = order == degree
                next_a = jnp.where(starts, first_a, rising * (x_a * now_a - falling * before_a))
                next_b = jnp.where(starts, first_b, rising * (x_b * now_b - falling * before_b))
                falling = gap * inverse_root * steps_ref[2, degree]
                now_a, before_a, now_b, before_b = next_a, now_a, next_b, now_b
                grown[0, pl.ds(at * DEG_SLOTS, DEG_SLOTS), :] = next_a
                grown[1, pl.ds(at * DEG_SLOTS, DEG_SLOTS), :] = next_b
            return now_a, before_a, now_b, before_b, falling

        state = lax.fori_loop(0, CHUNK // 8, advance, state)

        def lay_out(slot, carry, chunk=chunk):
            for half in range(2):
                legendre[
                    slot, chunk * CHUNK : chunk * CHUNK + CHUNK, half * 128 : half * 128 + 128
                ] = grown[half, pl.ds(slot, CHUNK, stride=DEG_SLOTS), :].astype(BF16)
            return carry

        lax.fori_loop(0, SLOTS, lay_out, 0)

    for lat in range(LDEV):
        wait_space(out_rows, in_rows, recv_sem, 0, lat)
        rows[lat] = in_rows[lat].astype(F32)
    for row in range(MAIN):
        stack = jnp.concatenate(
            [rows[lat, pl.ds(row, 64, stride=16), :] for lat in range(LDEV)]
            + [jnp.zeros((64, 128), F32)],
            axis=0,
        )
        turned = stack.T.astype(BF16)
        spread[row] = turned[0:96]
        if row < 6:
            at = 32 * (row % 3)
            spread[MAIN + row // 3, at : at + 32, :] = turned[96:128]
    load_gain.wait()

    def filter_slot(slot, carry):
        table = legendre[slot]
        spectrum = lax.dot_general(
            spread[slot], table, (((1,), (1,)), ((), ())), preferred_element_type=F32
        )
        real, imag = spectrum[0:CDEV], spectrum[CDEV:96]
        gain_real = gain_ref[slot, 0].astype(F32)
        gain_imag = gain_ref[slot, 1].astype(F32)
        filtered = jnp.concatenate(
            [gain_real * real - gain_imag * imag, gain_real * imag + gain_imag * real], axis=0
        ).astype(BF16)
        made[slot] = jnp.dot(filtered, table, preferred_element_type=F32)
        return carry

    lax.fori_loop(0, SLOTS, filter_slot, 0)
    for row in range(MAIN):
        extra = jnp.zeros((32, 256), F32)
        if row < 6:
            at = 32 * (row % 3)
            extra = made[MAIN + row // 3, at : at + 32, :]
        turned = jnp.concatenate([made[row], extra], axis=0).T
        for lat in range(LDEV):
            rows[lat, pl.ds(row, 64, stride=16), :] = turned[lat * 64 : lat * 64 + 64]
    for lat in range(LDEV):
        back_rows[lat] = rows[lat].astype(BF16)
        send_space(back_rows, got_rows, 1, lat)

    pltpu.make_async_copy(
        coefs.at[pl.ds(0, CHANS - 1)], coefs.at[pl.ds(0, CHANS - 1)], chan_recv.at[0]
    ).wait()
    for k in range(BASIS):
        turned = jnp.concatenate([coefs[g, k] for g in range(CHANS)], axis=0).astype(F32).T
        if k == 1:
            bias_ref[...] = jnp.broadcast_to(
                jnp.sum(turned, axis=1, keepdims=True), bias_ref.shape
            )
        else:
            at = (k if k == 0 else k - 1) * 384
            coef_ref[:, at : at + 384] = turned.astype(BF16)
    load_inverse.wait()

    for lat in range(LDEV):
        wait_space(back_rows, got_rows, recv_sem, 1, lat)
        rows[lat] = got_rows[lat].astype(F32)
        for pair in range(MAIN // 2):
            turned = jnp.concatenate(
                [rows[lat, pl.ds(pair * 2 + half, 64, stride=16), :] for half in range(2)], axis=0
            ).T
            gathered[:, pair * 128 : pair * 128 + 128] = turned[0:96].astype(BF16)
            if pair < 3:
                third = third_of(pair, (32, 128))
                for th in range(3):
                    gathered[
                        th * 32 : th * 32 + 32, 1024 + pair * 128 : 1024 + pair * 128 + 128
                    ] = jnp.where(third == th, turned[96:128], 0.0).astype(BF16)
        total = lax.dot_general(
            gathered[...], hot[...], (((1,), (1,)), ((), ())), preferred_element_type=F32
        )
        for k in range(2):
            modes[:, k * MPAD : (k + 1) * MPAD] = total[k * CDEV : k * CDEV + CDEV].astype(BF16)
        for block in range(12):
            lanes = slice(block * 128, block * 128 + 128)
            spatial = jnp.dot(modes[...], inverse_ref[:, lanes], preferred_element_type=F32)
            chip, inner = block // 3, block % 3
            if block < 11:
                old = x_ref[lat, :, lanes].astype(F32)
            else:
                old = jnp.concatenate(
                    [x_ref[lat, :, 1408:1440], jnp.zeros((CDEV, 96), BF16)], axis=1
                ).astype(F32)
            new = (old + spatial).astype(BF16)
            if lat == 0:
                places = [(2 * chip, inner)]
            elif lat == 2:
                places = [(2 * chip + 1, inner)]
            elif inner < 2:
                places = [(2 * chip, 3 + inner)]
            else:
                places = [(2 * chip + 1, 3), (2 * chip + 1, 4)]
            for part, at in places:
                updated[part, :, at * 128 : at * 128 + 128] = new
    send_chan(updated, whole, 1)
    wait_chan(updated, whole, chan_recv, 1)

    for block in range(5):
        lanes = slice(block * 128, block * 128 + 128)
        u = whole[:, :, lanes].reshape(384, 128).astype(F32)
        t = jnp.tanh(u)
        base = 0.5 * u * (1.0 + jnp.tanh(0.5 * u))
        second = 2.0 * t * t - 1.0
        third = 2.0 * t * second - t
        fourth = 2.0 * t * third - second
        basis = jnp.concatenate(
            [piece.astype(BF16) for piece in (base, t, second, third, fourth)], axis=0
        )
        total = jnp.dot(coef_ref[...], basis, preferred_element_type=F32)
        mixed[:, :, lanes] = (total + bias_ref[...]).astype(BF16).reshape(CHANS, CDEV, 128)
    send_chan(mixed, final, 2)
    wait_chan(mixed, final, chan_recv, 2)
    for block in range(12):
        chip, inner = block // 3, block % 3
        width = 128 if block < 11 else 32
        for lat in range(LDEV):
            if lat == 0:
                part, at = 2 * chip, inner
            elif lat == 2:
                part, at = 2 * chip + 1, inner
            elif inner < 2:
                part, at = 2 * chip, 3 + inner
            else:
                part, at = 2 * chip + 1, 3
            out_ref[lat, :, block * 128 : block * 128 + width] = final[
                part, :, at * 128 : at * 128 + width
            ]

    for lat in range(LDEV):
        wait_space(out_rows, in_rows, send_sem, 0, lat)
        wait_space(back_rows, got_rows, send_sem, 1, lat)
    pltpu.make_async_copy(
        coefs.at[pl.ds(0, CHANS - 1)], coefs.at[pl.ds(0, CHANS - 1)], chan_send.at[0]
    ).wait()
    wait_chan(updated, whole, chan_send, 1)
    wait_chan(mixed, final, chan_send, 2)


def shards(state_field, slot_wave, spectral_filter, kan_coef):
    forward, inverse, weights, xrow, first, steps = make_tables()
    x = jnp.transpose(state_field, (1, 0, 2))
    slots = slot_wave.reshape(SPACES, SLOTS)
    cols = jnp.concatenate(
        [slots[:, :MAIN].T.reshape(-1)] + [slots[:, 16]] * 3 + [slots[:, 17]] * 3
    )
    cols = jnp.broadcast_to(cols[None, :], (8, COLS))
    message = pltpu.VMEM((LDEV, SPACES * 16, 128), BF16)
    part = pltpu.VMEM((CHANS, CDEV, PART), BF16)
    out = pl.pallas_call(
        block_kernel,
        out_shape=jax.ShapeDtypeStruct((LDEV, CDEV, NLON), BF16),
        in_specs=[HBM] * 5 + [SMEM] * 3 + [VMEM] * 3,
        out_specs=VMEM,
        scratch_shapes=[
            pltpu.VMEM((LDEV, CDEV, NLON), BF16),
            pltpu.VMEM((2, NLON, MPAD), BF16),
            pltpu.VMEM((2 * MPAD, NPAD), BF16),
            pltpu.VMEM((SLOTS, 2, CDEV, LMAX), BF16),
            pltpu.VMEM((CHANS, BASIS, CDEV, 384), BF16),
            pltpu.SemaphoreType.DMA((5,)),
            pltpu.SemaphoreType.DMA((2, LDEV)),
            pltpu.SemaphoreType.DMA((2, LDEV)),
            pltpu.SemaphoreType.DMA((3,)),
            pltpu.SemaphoreType.DMA((3,)),
            pltpu.VMEM((MPAD, COLS), BF16),
            pltpu.VMEM((96, MPAD), BF16),
            pltpu.VMEM((96, COLS), F32),
            pltpu.VMEM((LDEV, SPACES * 16, 128), F32),
            message,
            message,
            pltpu.VMEM((DEG_SLOTS, 128), jnp.int32),
            pltpu.VMEM((DEG_SLOTS, 256), F32),
            pltpu.VMEM((2, CHUNK * DEG_SLOTS, 128), F32),
            pltpu.VMEM((SLOTS, LMAX, 256), BF16),
            pltpu.VMEM((SLOTS, 96, 256), BF16),
            pltpu.VMEM((SLOTS, 96, 256), F32),
            message,
            message,
            pltpu.VMEM((384, 5 * 384), BF16),
            pltpu.VMEM((384, 128), F32),
            pltpu.VMEM((96, COLS), BF16),
            pltpu.VMEM((CDEV, 2 * MPAD), BF16),
            part,
            part,
            part,
            part,
        ],
        compiler_params=pltpu.CompilerParams(
            collective_id=0, has_side_effects=True, vmem_limit_bytes=60 * 1024 * 1024
        ),
        name="spectral_block",
    )(x, forward, inverse, spectral_filter, kan_coef, slot_wave, weights, steps, cols, xrow, first)
    return jnp.transpose(out, (1, 0, 2))


def solution(mesh):
    in_specs = (
        P("chan", "space", None),
        P(),
        P("space", None, "chan", None),
        P(None, "chan", None),
    )
    out_specs = P("chan", "space", None)
    return jax.shard_map(shards, mesh=mesh, in_specs=in_specs, out_specs=out_specs, check_vma=False)
```

```python
import math

import jax
import jax.numpy as jnp
import ml_dtypes
import numpy as np
from jax import lax
from jax.experimental import pallas as pl
from jax.experimental.pallas import tpu as pltpu
from jax.sharding import PartitionSpec as P

NLON = 1440
MMAX = 720
LMAX = 720
BASIS = 6
MPAD = 768
NPAD = 1536
SLOTS = 18
MAIN = 16
SPACES = 64
CHANS = 8
CDEV = 48
LDEV = 3
LAT = 192
ROWS = 48
COLS = 1408
PART = 256
DEG_SLOTS = 24
CHUNK = 240
F32 = jnp.float32
BF16 = jnp.bfloat16

VMEM = pl.BlockSpec(memory_space=pltpu.VMEM)
SMEM = pl.BlockSpec(memory_space=pltpu.SMEM)
HBM = pl.BlockSpec(memory_space=pl.ANY)
MESH = pl.DeviceIdType.MESH


def make_tables():
    m = np.arange(MMAX)[:, None]
    n = np.arange(NLON)[None, :]
    angle = (m * n % NLON) * (2.0 * np.pi / NLON)
    cos, sin = np.cos(angle), np.sin(angle)
    forward = np.zeros((2, NLON, MPAD))
    forward[0, :, :MMAX] = cos.T / NLON
    forward[1, :, :MMAX] = -sin.T / NLON
    factor = np.where(m == 0, 1.0, 2.0)
    inverse = np.zeros((2 * MPAD, NPAD))
    inverse[:MMAX, :NLON] = factor * cos
    inverse[MPAD : MPAD + MMAX, :NLON] = -factor * sin
    lat = np.arange(LAT)
    colat = 0.5 * np.pi + (lat + 0.5 - 0.5 * LAT) * (np.pi / LMAX)
    weights = (2.0 * np.pi * np.pi / LMAX * np.sin(colat)).astype(np.float32)
    order = (3 * np.arange(SPACES)[None, :] + np.arange(LDEV)[:, None]).reshape(-1)
    xrow = np.zeros((8, 256), np.float32)
    xrow[:, :LAT] = np.cos(colat)[order]
    first = np.zeros((MMAX + 8, 256), np.float32)
    for wave in range(MMAX):
        base = 0.5 * (
            math.log((2.0 * wave + 1.0) / (4.0 * math.pi))
            + math.lgamma(wave + 0.5)
            - math.lgamma(wave + 1.0)
            - 0.5 * math.log(math.pi)
        )
        first[wave, :LAT] = np.exp(base + wave * np.log(np.sin(colat)))[order]
    degree = np.arange(LMAX, dtype=np.float64)
    root = np.sqrt(np.maximum(4.0 * degree * degree - 1.0, 1.0))
    steps = np.stack([degree * degree, root, 1.0 / root]).astype(np.float32)
    return (
        forward.astype(ml_dtypes.bfloat16),
        inverse.astype(ml_dtypes.bfloat16),
        weights,
        xrow,
        first,
        steps,
    )


def one_hot(cols_row, start, size):
    waves = lax.broadcasted_iota(jnp.int32, (MPAD, size), 0)
    return jnp.where(waves == cols_row[0:1, start : start + size], 1.0, 0.0).astype(BF16)


def third_of(pair, shape):
    lane = lax.broadcasted_iota(jnp.int32, shape, 1)
    return jnp.where(lane >= 64, (2 * pair + 1) % 3, (2 * pair) % 3)


def far(i):
    return 4 + ((i + 1) // 2) * (1 - 2 * (i % 2))


def places(lat, block):
    chip, inner = block // 3, block % 3
    if lat == 1:
        return [[(2 * chip, 0), (2 * chip, 1)], [(2 * chip + 1, 0)], [(2 * chip + 1, 1)]][inner]
    return [[(2 * chip, 0)], [(2 * chip, 1)], [(2 * chip + 1, 0), (2 * chip + 1, 1)]][inner]


def block_kernel(
    x_hbm,
    forward_hbm,
    inverse_hbm,
    gain_hbm,
    coef_hbm,
    wave_ref,
    weight_ref,
    steps_ref,
    cols_ref,
    xrow_ref,
    first_ref,
    out_ref,
    x_ref,
    forward_ref,
    inverse_ref,
    gain_ref,
    coefs,
    load_sem,
    send_sem,
    recv_sem,
    chan_send,
    chan_recv,
    coef_send,
    coef_recv,
    hot,
    zonal,
    packed,
    rows,
    out_rows,
    in_rows,
    order_ref,
    start_ref,
    grown,
    legendre,
    spread,
    made,
    back_rows,
    got_rows,
    coef_ref,
    bias_ref,
    gathered,
    modes,
    basis,
    updated,
    whole,
    mixed,
    final,
):
    here = lax.axis_index("space")
    group = lax.axis_index("chan")
    here_y, here_z = here // 8, here % 8
    chip, core = group // 2, group % 2
    sibling = chip * 2 + 1 - core

    def space_peer(k):
        return lax.rem(here_y + far(k // 8), 8) * 8 + lax.rem(here_z + far(k % 8), 8)

    loads = [
        pltpu.make_async_copy(source, target, load_sem.at[i])
        for i, (source, target) in enumerate(
            (
                (x_hbm, x_ref),
                (forward_hbm, forward_ref),
                (inverse_hbm, inverse_ref),
                (gain_hbm, gain_ref),
                (coef_hbm, coefs.at[core, chip]),
            )
        )
    ]
    load_x, load_forward, load_inverse, load_gain, load_coef = loads
    for load in loads:
        load.start()

    barrier = pltpu.get_barrier_semaphore()

    def greet_space(k, carry):
        pl.semaphore_signal(
            barrier, inc=1, device_id={"space": space_peer(k)}, device_id_type=MESH
        )
        return carry

    def greet_chan(k, carry):
        pl.semaphore_signal(
            barrier, inc=1, device_id={"chan": lax.rem(group + k, CHANS)}, device_id_type=MESH
        )
        return carry

    lax.fori_loop(0, SPACES - 1, greet_space, 0)
    lax.fori_loop(1, CHANS, greet_chan, 0)

    def send_space(source, target, step, lat):
        def one(k, carry):
            peer = space_peer(k)
            pltpu.make_async_remote_copy(
                src_ref=source.at[lat, pl.ds(pl.multiple_of(peer * 16, 16), 16)],
                dst_ref=target.at[lat, pl.ds(pl.multiple_of(here * 16, 16), 16)],
                send_sem=send_sem.at[step, lat],
                recv_sem=recv_sem.at[step, lat],
                device_id={"space": peer},
                device_id_type=MESH,
            ).start()
            return carry

        lax.fori_loop(0, SPACES - 1, one, 0)
        own = pl.ds(pl.multiple_of(here * 16, 16), 16)
        target[lat, own, :] = source[lat, own, :]

    def wait_space(source, target, sem, step, lat):
        most = pl.ds(0, (SPACES - 1) * 16)
        pltpu.make_async_copy(
            source.at[lat, most], target.at[lat, most], sem.at[step, lat]
        ).wait()

    def send_chan(source, target, step, lat):
        def one(k, carry):
            peer = lax.rem(group + far(k), CHANS)
            pltpu.make_async_remote_copy(
                src_ref=source.at[lat, peer],
                dst_ref=target.at[lat, group],
                send_sem=chan_send.at[step, lat],
                recv_sem=chan_recv.at[step, lat],
                device_id={"chan": peer},
                device_id_type=MESH,
            ).start()
            return carry

        lax.fori_loop(0, CHANS - 1, one, 0)
        target[lat, group] = source[lat, group]

    def wait_chan(source, target, sem, step, lat):
        most = pl.ds(0, CHANS - 1)
        pltpu.make_async_copy(
            source.at[lat, most], target.at[lat, most], sem.at[step, lat]
        ).wait()

    def send_coef(k, carry):
        pltpu.make_async_remote_copy(
            src_ref=coefs.at[core, chip],
            dst_ref=coefs.at[core, chip],
            send_sem=coef_send.at[0],
            recv_sem=coef_recv.at[0],
            device_id={"chan": lax.rem(group + 2 * k, CHANS)},
            device_id_type=MESH,
        ).start()
        return carry

    def wait_coef(count, sem):
        most = pl.ds(0, count)
        pltpu.make_async_copy(coefs.at[0, most], coefs.at[0, most], sem).wait()

    cols = cols_ref[...]
    for start in range(0, COLS, 128):
        hot[:, start : start + 128] = one_hot(cols, start, 128)
    load_x.wait()
    load_forward.wait()
    for lat in range(LDEV):
        weight = weight_ref[here * LDEV + lat]
        for k in range(2):
            part = jnp.dot(x_ref[lat], forward_ref[k], preferred_element_type=F32)
            zonal[k * CDEV : k * CDEV + CDEV, :] = (part * weight).astype(BF16)
        packed[...] = jnp.dot(zonal[...], hot[...], preferred_element_type=F32)
        for pair in range(MAIN // 2):
            main = packed[:, pair * 128 : pair * 128 + 128]
            extra = jnp.zeros((32, 128), F32)
            if pair < 3:
                wide = packed[:, 1024 + pair * 128 : 1024 + pair * 128 + 128]
                third = third_of(pair, (32, 128))
                for th in range(3):
                    extra = jnp.where(third == th, wide[th * 32 : th * 32 + 32], extra)
            turned = jnp.concatenate([main, extra], axis=0).T
            for half in range(2):
                rows[lat, pl.ds(pair * 2 + half, 64, stride=16), :] = turned[
                    half * 64 : half * 64 + 64
                ]
        out_rows[lat] = rows[lat].astype(BF16)
        if lat == 0:
            pl.semaphore_wait(barrier, SPACES - 1 + CHANS - 1)
        send_space(out_rows, in_rows, 0, lat)
        if lat == 0:
            load_coef.wait()
            lax.fori_loop(1, 4, send_coef, 0)


    for slot in range(DEG_SLOTS):
        wave = wave_ref[here * SLOTS + slot] if slot < SLOTS else MMAX
        order_ref[slot : slot + 1, :] = jnp.full((1, 128), wave, jnp.int32)
        start_ref[slot : slot + 1, :] = first_ref[pl.ds(wave, 1), :]
    order = order_ref[...]
    square = order.astype(F32) * order.astype(F32)
    first_a, first_b = start_ref[:, 0:128], start_ref[:, 128:256]
    x_a = jnp.broadcast_to(xrow_ref[0:1, 0:128], (DEG_SLOTS, 128))
    x_b = jnp.broadcast_to(xrow_ref[0:1, 128:256], (DEG_SLOTS, 128))
    zero = jnp.zeros((DEG_SLOTS, 128), F32)
    state = (zero, zero, zero, zero, zero)
    for chunk in range(LMAX // CHUNK):

        def advance(block, carry, chunk=chunk):
            now_a, before_a, now_b, before_b, falling = carry
            for offset in range(8):
                at = block * 8 + offset
                degree = chunk * CHUNK + at
                gap = steps_ref[0, degree] - square
                inverse_root = lax.rsqrt(jnp.maximum(gap, 1.0))
                rising = steps_ref[1, degree] * inverse_root
                starts = order == degree
                next_a = jnp.where(starts, first_a, rising * (x_a * now_a - falling * before_a))
                next_b = jnp.where(starts, first_b, rising * (x_b * now_b - falling * before_b))
                falling = gap * inverse_root * steps_ref[2, degree]
                now_a, before_a, now_b, before_b = next_a, now_a, next_b, now_b
                grown[0, pl.ds(at * DEG_SLOTS, DEG_SLOTS), :] = next_a
                grown[1, pl.ds(at * DEG_SLOTS, DEG_SLOTS), :] = next_b
            return now_a, before_a, now_b, before_b, falling

        state = lax.fori_loop(0, CHUNK // 8, advance, state)

        def lay_out(slot, carry, chunk=chunk):
            for half in range(2):
                legendre[
                    slot, chunk * CHUNK : chunk * CHUNK + CHUNK, half * 128 : half * 128 + 128
                ] = grown[half, pl.ds(slot, CHUNK, stride=DEG_SLOTS), :].astype(BF16)
            return carry

        lax.fori_loop(0, SLOTS, lay_out, 0)

    wait_coef(3, coef_recv.at[0])
    pltpu.make_async_remote_copy(
        src_ref=coefs.at[core],
        dst_ref=coefs.at[core],
        send_sem=coef_send.at[1],
        recv_sem=coef_recv.at[1],
        device_id={"chan": sibling},
        device_id_type=MESH,
    ).start()

    for lat in range(LDEV):
        wait_space(out_rows, in_rows, recv_sem, 0, lat)
        rows[lat] = in_rows[lat].astype(F32)
    for row in range(MAIN):
        stack = jnp.concatenate(
            [rows[lat, pl.ds(row, 64, stride=16), :] for lat in range(LDEV)]
            + [jnp.zeros((64, 128), F32)],
            axis=0,
        )
        turned = stack.T.astype(BF16)
        spread[row] = turned[0:96]
        if row < 6:
            at = 32 * (row % 3)
            spread[MAIN + row // 3, at : at + 32, :] = turned[96:128]
    load_gain.wait()

    def filter_slots(step, carry):
        slots = [step * 3 + i for i in range(3)]
        spectra = [
            lax.dot_general(
                spread[slot], legendre[slot], (((1,), (1,)), ((), ())), preferred_element_type=F32
            )
            for slot in slots
        ]
        for slot, spectrum in zip(slots, spectra):
            real, imag = spectrum[0:CDEV], spectrum[CDEV:96]
            gain_real = gain_ref[slot, 0].astype(F32)
            gain_imag = gain_ref[slot, 1].astype(F32)
            filtered = jnp.concatenate(
                [gain_real * real - gain_imag * imag, gain_real * imag + gain_imag * real], axis=0
            ).astype(BF16)
            made[slot] = jnp.dot(filtered, legendre[slot], preferred_element_type=F32)
        return carry

    lax.fori_loop(0, SLOTS // 3, filter_slots, 0)
    for row in range(MAIN):
        extra = jnp.zeros((32, 256), F32)
        if row < 6:
            at = 32 * (row % 3)
            extra = made[MAIN + row // 3, at : at + 32, :]
        turned = jnp.concatenate([made[row], extra], axis=0).T
        for lat in range(LDEV):
            rows[lat, pl.ds(row, 64, stride=16), :] = turned[lat * 64 : lat * 64 + 64]
    for lat in range(LDEV):
        back_rows[lat] = rows[lat].astype(BF16)
        send_space(back_rows, got_rows, 1, lat)

    wait_coef(4, coef_recv.at[1])
    for k in range(BASIS):
        turned = jnp.concatenate(
            [coefs[g % 2, g // 2, k] for g in range(CHANS)], axis=0
        ).astype(F32).T
        if k == 1:
            bias_ref[...] = jnp.broadcast_to(
                jnp.sum(turned, axis=1, keepdims=True), bias_ref.shape
            )
        else:
            at = (k if k == 0 else k - 1) * 384
            coef_ref[:, at : at + 384] = turned.astype(BF16)
    load_inverse.wait()

    def mix(lat):
        wait_chan(updated, whole, chan_recv, 0, lat)
        u = whole[lat].reshape(384, PART).astype(F32)
        t = jnp.tanh(u)
        base = 0.5 * u * (1.0 + jnp.tanh(0.5 * u))
        second = 2.0 * t * t - 1.0
        third = 2.0 * t * second - t
        fourth = 2.0 * t * third - second
        for k, piece in enumerate((base, t, second, third, fourth)):
            basis[k * 384 : k * 384 + 384, :] = piece.astype(BF16)
        for half in range(2):
            total = jnp.dot(
                coef_ref[half * 192 : half * 192 + 192, :], basis[...], preferred_element_type=F32
            )
            bias = bias_ref[half * 192 : half * 192 + 192, 0:1]
            mixed[lat, half * 4 : half * 4 + 4] = (
                (total + bias).astype(BF16).reshape(4, CDEV, PART)
            )
        send_chan(mixed, final, 1, lat)

    for lat in range(LDEV):
        wait_space(back_rows, got_rows, recv_sem, 1, lat)
        rows[lat] = got_rows[lat].astype(F32)
        for pair in range(MAIN // 2):
            turned = jnp.concatenate(
                [rows[lat, pl.ds(pair * 2 + half, 64, stride=16), :] for half in range(2)], axis=0
            ).T
            gathered[:, pair * 128 : pair * 128 + 128] = turned[0:96].astype(BF16)
            if pair < 3:
                third = third_of(pair, (32, 128))
                for th in range(3):
                    gathered[
                        th * 32 : th * 32 + 32, 1024 + pair * 128 : 1024 + pair * 128 + 128
                    ] = jnp.where(third == th, turned[96:128], 0.0).astype(BF16)
        total = lax.dot_general(
            gathered[...], hot[...], (((1,), (1,)), ((), ())), preferred_element_type=F32
        )
        for k in range(2):
            modes[:, k * MPAD : (k + 1) * MPAD] = total[k * CDEV : k * CDEV + CDEV].astype(BF16)
        for strip in range(6):
            spatial = jnp.dot(
                modes[...],
                inverse_ref[:, strip * 256 : strip * 256 + 256],
                preferred_element_type=F32,
            )
            for block in (2 * strip, 2 * strip + 1):
                lanes = slice(block * 128, block * 128 + 128)
                if block < 11:
                    old = x_ref[lat, :, lanes].astype(F32)
                else:
                    old = jnp.concatenate(
                        [x_ref[lat, :, 1408:1440], jnp.zeros((CDEV, 96), BF16)], axis=1
                    ).astype(F32)
                at = (block % 2) * 128
                new = (old + spatial[:, at : at + 128]).astype(BF16)
                for part, place in places(lat, block):
                    updated[lat, part, :, place * 128 : place * 128 + 128] = new
        send_chan(updated, whole, 0, lat)
        if lat > 0:
            mix(lat - 1)
    mix(LDEV - 1)
    for lat in range(LDEV):
        wait_chan(mixed, final, chan_recv, 1, lat)
        for block in range(12):
            part, place = places(lat, block)[0]
            width = 128 if block < 11 else 32
            out_ref[lat, :, block * 128 : block * 128 + width] = final[
                lat, part, :, place * 128 : place * 128 + width
            ]

    for lat in range(LDEV):
        wait_space(out_rows, in_rows, send_sem, 0, lat)
        wait_space(back_rows, got_rows, send_sem, 1, lat)
        wait_chan(updated, whole, chan_send, 0, lat)
        wait_chan(mixed, final, chan_send, 1, lat)
    wait_coef(3, coef_send.at[0])
    wait_coef(4, coef_send.at[1])


def shards(state_field, slot_wave, spectral_filter, kan_coef):
    forward, inverse, weights, xrow, first, steps = make_tables()
    x = jnp.transpose(state_field, (1, 0, 2))
    slots = slot_wave.reshape(SPACES, SLOTS)
    cols = jnp.concatenate(
        [slots[:, :MAIN].T.reshape(-1)] + [slots[:, 16]] * 3 + [slots[:, 17]] * 3
    )
    cols = jnp.broadcast_to(cols[None, :], (8, COLS))
    message = pltpu.VMEM((LDEV, SPACES * 16, 128), BF16)
    part = pltpu.VMEM((LDEV, CHANS, CDEV, PART), BF16)
    out = pl.pallas_call(
        block_kernel,
        out_shape=jax.ShapeDtypeStruct((LDEV, CDEV, NLON), BF16),
        in_specs=[HBM] * 5 + [SMEM] * 3 + [VMEM] * 3,
        out_specs=VMEM,
        scratch_shapes=[
            pltpu.VMEM((LDEV, CDEV, NLON), BF16),
            pltpu.VMEM((2, NLON, MPAD), BF16),
            pltpu.VMEM((2 * MPAD, NPAD), BF16),
            pltpu.VMEM((SLOTS, 2, CDEV, LMAX), BF16),
            pltpu.VMEM((2, CHANS // 2, BASIS, CDEV, 384), BF16),
            pltpu.SemaphoreType.DMA((5,)),
            pltpu.SemaphoreType.DMA((2, LDEV)),
            pltpu.SemaphoreType.DMA((2, LDEV)),
            pltpu.SemaphoreType.DMA((2, LDEV)),
            pltpu.SemaphoreType.DMA((2, LDEV)),
            pltpu.SemaphoreType.DMA((2,)),
            pltpu.SemaphoreType.DMA((2,)),
            pltpu.VMEM((MPAD, COLS), BF16),
            pltpu.VMEM((96, MPAD), BF16),
            pltpu.VMEM((96, COLS), F32),
            pltpu.VMEM((LDEV, SPACES * 16, 128), F32),
            message,
            message,
            pltpu.VMEM((DEG_SLOTS, 128), jnp.int32),
            pltpu.VMEM((DEG_SLOTS, 256), F32),
            pltpu.VMEM((2, CHUNK * DEG_SLOTS, 128), F32),
            pltpu.VMEM((SLOTS, LMAX, 256), BF16),
            pltpu.VMEM((SLOTS, 96, 256), BF16),
            pltpu.VMEM((SLOTS, 96, 256), F32),
            message,
            message,
            pltpu.VMEM((384, 5 * 384), BF16),
            pltpu.VMEM((384, 128), F32),
            pltpu.VMEM((96, COLS), BF16),
            pltpu.VMEM((CDEV, 2 * MPAD), BF16),
            pltpu.VMEM((5 * 384, PART), BF16),
            part,
            part,
            part,
            part,
        ],
        compiler_params=pltpu.CompilerParams(
            collective_id=0, has_side_effects=True, vmem_limit_bytes=60 * 1024 * 1024
        ),
        name="spectral_block",
    )(x, forward, inverse, spectral_filter, kan_coef, slot_wave, weights, steps, cols, xrow, first)
    return jnp.transpose(out, (1, 0, 2))


def solution(mesh):
    in_specs = (
        P("chan", "space", None),
        P(),
        P("space", None, "chan", None),
        P(None, "chan", None),
    )
    out_specs = P("chan", "space", None)
    return jax.shard_map(shards, mesh=mesh, in_specs=in_specs, out_specs=out_specs, check_vma=False)
```

```python
import math

import jax
import jax.numpy as jnp
import ml_dtypes
import numpy as np
from jax import lax
from jax.experimental import pallas as pl
from jax.experimental.pallas import tpu as pltpu
from jax.sharding import PartitionSpec as P

NLON = 1440
MMAX = 720
LMAX = 720
BASIS = 6
MPAD = 768
NPAD = 1536
SLOTS = 18
MAIN = 16
SPACES = 64
CHANS = 8
CDEV = 48
LDEV = 3
LAT = 192
ROWS = 48
COLS = 1152
PART = 256
DEG_SLOTS = 24
CHUNK = 240
F32 = jnp.float32
BF16 = jnp.bfloat16

VMEM = pl.BlockSpec(memory_space=pltpu.VMEM)
SMEM = pl.BlockSpec(memory_space=pltpu.SMEM)
HBM = pl.BlockSpec(memory_space=pl.ANY)
MESH = pl.DeviceIdType.MESH


def make_tables():
    m = np.arange(MMAX)[:, None]
    n = np.arange(NLON)[None, :]
    angle = (m * n % NLON) * (2.0 * np.pi / NLON)
    cos, sin = np.cos(angle), np.sin(angle)
    forward = np.zeros((2, NLON, MPAD))
    forward[0, :, :MMAX] = cos.T / NLON
    forward[1, :, :MMAX] = -sin.T / NLON
    factor = np.where(m == 0, 1.0, 2.0)
    inverse = np.zeros((2 * MPAD, NPAD))
    inverse[:MMAX, :NLON] = factor * cos
    inverse[MPAD : MPAD + MMAX, :NLON] = -factor * sin
    lat = np.arange(LAT)
    colat = 0.5 * np.pi + (lat + 0.5 - 0.5 * LAT) * (np.pi / LMAX)
    weights = (2.0 * np.pi * np.pi / LMAX * np.sin(colat)).astype(np.float32)
    order = (3 * np.arange(SPACES)[None, :] + np.arange(LDEV)[:, None]).reshape(-1)
    xrow = np.zeros((8, 256), np.float32)
    xrow[:, :LAT] = np.cos(colat)[order]
    first = np.zeros((MMAX + 8, 256), np.float32)
    for wave in range(MMAX):
        base = 0.5 * (
            math.log((2.0 * wave + 1.0) / (4.0 * math.pi))
            + math.lgamma(wave + 0.5)
            - math.lgamma(wave + 1.0)
            - 0.5 * math.log(math.pi)
        )
        first[wave, :LAT] = np.exp(base + wave * np.log(np.sin(colat)))[order]
    degree = np.arange(LMAX, dtype=np.float64)
    root = np.sqrt(np.maximum(4.0 * degree * degree - 1.0, 1.0))
    steps = np.stack([degree * degree, root, 1.0 / root]).astype(np.float32)
    return (
        forward.astype(ml_dtypes.bfloat16),
        inverse.astype(ml_dtypes.bfloat16),
        weights,
        xrow,
        first,
        steps,
    )


def one_hot(cols_row, start, size):
    waves = lax.broadcasted_iota(jnp.int32, (MPAD, size), 0)
    return jnp.where(waves == cols_row[0:1, start : start + size], 1.0, 0.0).astype(BF16)


ORDER = sorted(
    ((k // 8, k % 8) for k in range(1, SPACES)),
    key=lambda step: -min(step[0], 8 - step[0]) - min(step[1], 8 - step[1]),
)


def far(i):
    return 4 + ((i + 1) // 2) * (1 - 2 * (i % 2))


def places(lat, block):
    chip, inner = block // 3, block % 3
    if lat == 1:
        return [[(2 * chip, 0), (2 * chip, 1)], [(2 * chip + 1, 0)], [(2 * chip + 1, 1)]][inner]
    return [[(2 * chip, 0)], [(2 * chip, 1)], [(2 * chip + 1, 0), (2 * chip + 1, 1)]][inner]


def block_kernel(
    x_hbm,
    forward_hbm,
    inverse_hbm,
    gain_hbm,
    coef_hbm,
    wave_ref,
    weight_ref,
    steps_ref,
    cols_ref,
    xrow_ref,
    first_ref,
    final,
    x_ref,
    forward_ref,
    inverse_ref,
    gain_ref,
    coefs,
    load_sem,
    send_sem,
    recv_sem,
    chan_send,
    chan_recv,
    coef_send,
    coef_recv,
    hot,
    zonal,
    packed,
    flat,
    rows,
    out_rows,
    in_rows,
    order_ref,
    start_ref,
    grown,
    legendre,
    spread,
    made,
    back_rows,
    got_rows,
    coef_ref,
    bias_ref,
    gathered,
    modes,
    basis,
    updated,
    whole,
    mixed,
):
    here = lax.axis_index("space")
    group = lax.axis_index("chan")
    here_y, here_z = here // 8, here % 8
    chip, core = group // 2, group % 2
    sibling = chip * 2 + 1 - core

    def space_peer(k):
        return lax.rem(here_y + far(k // 8), 8) * 8 + lax.rem(here_z + far(k % 8), 8)

    loads = [
        pltpu.make_async_copy(source, target, load_sem.at[i])
        for i, (source, target) in enumerate(
            (
                (x_hbm, x_ref),
                (forward_hbm, forward_ref),
                (inverse_hbm, inverse_ref),
                (gain_hbm, gain_ref),
                (coef_hbm, coefs.at[core, chip]),
            )
        )
    ]
    load_x, load_forward, load_inverse, load_gain, load_coef = loads
    load_x.start()
    load_forward.start()

    barrier = pltpu.get_barrier_semaphore()

    def greet_space(k, carry):
        pl.semaphore_signal(
            barrier, inc=1, device_id={"space": space_peer(k)}, device_id_type=MESH
        )
        return carry

    def greet_chan(k, carry):
        pl.semaphore_signal(
            barrier, inc=1, device_id={"chan": lax.rem(group + k, CHANS)}, device_id_type=MESH
        )
        return carry

    lax.fori_loop(0, SPACES - 1, greet_space, 0)
    lax.fori_loop(1, CHANS, greet_chan, 0)

    def send_space(source, target, step, lat):
        for oy, oz in ORDER:
            peer = lax.rem(here_y + oy, 8) * 8 + lax.rem(here_z + oz, 8)
            pltpu.make_async_remote_copy(
                src_ref=source.at[lat, pl.ds(pl.multiple_of(peer * 16, 16), 16)],
                dst_ref=target.at[lat, pl.ds(pl.multiple_of(here * 16, 16), 16)],
                send_sem=send_sem.at[step, lat],
                recv_sem=recv_sem.at[step, lat],
                device_id={"space": peer},
                device_id_type=MESH,
            ).start()
        own = pl.ds(pl.multiple_of(here * 16, 16), 16)
        target[lat, own, :] = source[lat, own, :]

    def wait_space(source, target, sem, step, lat):
        most = pl.ds(0, (SPACES - 1) * 16)
        pltpu.make_async_copy(
            source.at[lat, most], target.at[lat, most], sem.at[step, lat]
        ).wait()

    def send_chan(source, target, step, lat):
        def one(k, carry):
            peer = lax.rem(group + far(k), CHANS)
            pltpu.make_async_remote_copy(
                src_ref=source.at[lat, peer],
                dst_ref=target.at[lat, group],
                send_sem=chan_send.at[step, lat],
                recv_sem=chan_recv.at[step, lat],
                device_id={"chan": peer},
                device_id_type=MESH,
            ).start()
            return carry

        lax.fori_loop(0, CHANS - 1, one, 0)
        target[lat, group] = source[lat, group]

    def wait_chan(source, target, sem, step, lat):
        most = pl.ds(0, CHANS - 1)
        pltpu.make_async_copy(
            source.at[lat, most], target.at[lat, most], sem.at[step, lat]
        ).wait()

    def send_coef(k, carry):
        pltpu.make_async_remote_copy(
            src_ref=coefs.at[core, chip],
            dst_ref=coefs.at[core, chip],
            send_sem=coef_send.at[0],
            recv_sem=coef_recv.at[0],
            device_id={"chan": lax.rem(group + 2 * k, CHANS)},
            device_id_type=MESH,
        ).start()
        return carry

    def wait_coef(count, sem):
        most = pl.ds(0, count)
        pltpu.make_async_copy(coefs.at[0, most], coefs.at[0, most], sem).wait()

    lane = lax.broadcasted_iota(jnp.int32, (64, 128), 1)
    tail_lane = lane >= 96
    flat[...] = jnp.zeros_like(flat)
    cols = cols_ref[...]
    for start in range(0, COLS, 128):
        hot[:, start : start + 128] = one_hot(cols, start, 128)
    load_x.wait()
    load_forward.wait()
    for load in (load_coef, load_gain, load_inverse):
        load.start()
    for lat in range(LDEV):
        weight = weight_ref[here * LDEV + lat]
        for k in range(2):
            part = jnp.dot(x_ref[lat], forward_ref[k], preferred_element_type=F32)
            zonal[k * CDEV : k * CDEV + CDEV, :] = (part * weight).astype(BF16)
        packed[...] = jnp.dot(zonal[...], hot[...], preferred_element_type=F32)
        for start in range(0, COLS, 128):
            flat[start : start + 128, 0:96] = packed[:, start : start + 128].T
        for row in range(MAIN):
            line = flat[pl.ds(row, 64, stride=SLOTS), :]
            if row < 6:
                last = flat[pl.ds(MAIN + row // 3, 64, stride=SLOTS), :]
                line = jnp.where(tail_lane, pltpu.roll(last, 96 - 32 * (row % 3), 1), line)
            rows[lat, pl.ds(row, 64, stride=16), :] = line
        out_rows[lat] = rows[lat].astype(BF16)
        if lat == 0:
            pl.semaphore_wait(barrier, SPACES - 1 + CHANS - 1)
        send_space(out_rows, in_rows, 0, lat)
        if lat == 0:
            load_coef.wait()
            lax.fori_loop(1, 4, send_coef, 0)


    for slot in range(DEG_SLOTS):
        wave = wave_ref[here * SLOTS + slot] if slot < SLOTS else MMAX
        order_ref[slot : slot + 1, :] = jnp.full((1, 128), wave, jnp.int32)
        start_ref[slot : slot + 1, :] = first_ref[pl.ds(wave, 1), :]
    order = order_ref[...]
    square = order.astype(F32) * order.astype(F32)
    first_a, first_b = start_ref[:, 0:128], start_ref[:, 128:256]
    x_a = jnp.broadcast_to(xrow_ref[0:1, 0:128], (DEG_SLOTS, 128))
    x_b = jnp.broadcast_to(xrow_ref[0:1, 128:256], (DEG_SLOTS, 128))
    zero = jnp.zeros((DEG_SLOTS, 128), F32)
    state = (zero, zero, zero, zero, zero)
    for chunk in range(LMAX // CHUNK):

        def advance(block, carry, chunk=chunk):
            now_a, before_a, now_b, before_b, falling = carry
            for offset in range(8):
                at = block * 8 + offset
                degree = chunk * CHUNK + at
                gap = steps_ref[0, degree] - square
                inverse_root = lax.rsqrt(jnp.maximum(gap, 1.0))
                rising = steps_ref[1, degree] * inverse_root
                starts = order == degree
                next_a = jnp.where(starts, first_a, rising * (x_a * now_a - falling * before_a))
                next_b = jnp.where(starts, first_b, rising * (x_b * now_b - falling * before_b))
                falling = gap * inverse_root * steps_ref[2, degree]
                now_a, before_a, now_b, before_b = next_a, now_a, next_b, now_b
                grown[0, pl.ds(at * DEG_SLOTS, DEG_SLOTS), :] = next_a
                grown[1, pl.ds(at * DEG_SLOTS, DEG_SLOTS), :] = next_b
            return now_a, before_a, now_b, before_b, falling

        state = lax.fori_loop(0, CHUNK // 8, advance, state)

        def lay_out(slot, carry, chunk=chunk):
            for half in range(2):
                legendre[
                    slot, chunk * CHUNK : chunk * CHUNK + CHUNK, half * 128 : half * 128 + 128
                ] = grown[half, pl.ds(slot, CHUNK, stride=DEG_SLOTS), :].astype(BF16)
            return carry

        lax.fori_loop(0, SLOTS, lay_out, 0)

    for lats in ((0, 1), (2,)):
        for lat in lats:
            wait_space(out_rows, in_rows, recv_sem, 0, lat)
            rows[lat] = in_rows[lat].astype(F32)
        lanes = slice(lats[0] * 64, lats[0] * 64 + 128)
        for row in range(MAIN):
            stack = [rows[lat, pl.ds(row, 64, stride=16), :] for lat in lats]
            if len(lats) == 1:
                stack.append(jnp.zeros((64, 128), F32))
            turned = jnp.concatenate(stack, axis=0).T.astype(BF16)
            spread[row, :, lanes] = turned[0:96]
            if row < 6:
                at = 32 * (row % 3)
                spread[MAIN + row // 3, at : at + 32, lanes] = turned[96:128]
    load_gain.wait()

    def filter_slots(step, carry):
        slots = [step * 6 + i for i in range(6)]
        spectra = [
            lax.dot_general(
                spread[slot], legendre[slot], (((1,), (1,)), ((), ())), preferred_element_type=F32
            )
            for slot in slots
        ]
        for slot, spectrum in zip(slots, spectra):
            real, imag = spectrum[0:CDEV], spectrum[CDEV:96]
            gain_real = gain_ref[slot, 0].astype(F32)
            gain_imag = gain_ref[slot, 1].astype(F32)
            filtered = jnp.concatenate(
                [gain_real * real - gain_imag * imag, gain_real * imag + gain_imag * real], axis=0
            ).astype(BF16)
            made[slot] = jnp.dot(filtered, legendre[slot], preferred_element_type=F32)
        return carry

    lax.fori_loop(0, SLOTS // 6, filter_slots, 0)
    for lats in ((0, 1), (2,)):
        lanes = slice(lats[0] * 64, lats[0] * 64 + 128)
        for row in range(MAIN):
            extra = jnp.zeros((32, 128), F32)
            if row < 6:
                at = 32 * (row % 3)
                extra = made[MAIN + row // 3, at : at + 32, lanes]
            turned = jnp.concatenate([made[row, :, lanes], extra], axis=0).T
            for i, lat in enumerate(lats):
                rows[lat, pl.ds(row, 64, stride=16), :] = turned[i * 64 : i * 64 + 64]
        for lat in lats:
            back_rows[lat] = rows[lat].astype(BF16)
            send_space(back_rows, got_rows, 1, lat)

    wait_coef(3, coef_recv.at[0])
    pltpu.make_async_remote_copy(
        src_ref=coefs.at[core],
        dst_ref=coefs.at[core],
        send_sem=coef_send.at[1],
        recv_sem=coef_recv.at[1],
        device_id={"chan": sibling},
        device_id_type=MESH,
    ).start()

    load_inverse.wait()

    def mix(lat):
        wait_chan(updated, whole, chan_recv, 0, lat)
        u = whole[lat].reshape(384, PART).astype(F32)
        t = jnp.tanh(u)
        base = 0.5 * u * (1.0 + jnp.tanh(0.5 * u))
        second = 2.0 * t * t - 1.0
        third = 2.0 * t * second - t
        fourth = 2.0 * t * third - second
        for k, piece in enumerate((base, t, second, third, fourth)):
            basis[k * 384 : k * 384 + 384, :] = piece.astype(BF16)
        for half in range(2):
            total = jnp.dot(
                coef_ref[half * 192 : half * 192 + 192, :], basis[...], preferred_element_type=F32
            )
            bias = bias_ref[half * 192 : half * 192 + 192, 0:1]
            mixed[lat, half * 4 : half * 4 + 4] = (
                (total + bias).astype(BF16).reshape(4, CDEV, PART)
            )
        send_chan(mixed, final, 1, lat)

    def prepare_coef():
        wait_coef(4, coef_recv.at[1])
        for k in range(BASIS):
            turned = jnp.concatenate(
                [coefs[g % 2, g // 2, k] for g in range(CHANS)], axis=0
            ).astype(F32).T
            if k == 1:
                bias_ref[...] = jnp.broadcast_to(
                    jnp.sum(turned, axis=1, keepdims=True), bias_ref.shape
                )
            else:
                at = (k if k == 0 else k - 1) * 384
                coef_ref[:, at : at + 384] = turned.astype(BF16)

    for lat in range(LDEV):
        wait_space(back_rows, got_rows, recv_sem, 1, lat)
        rows[lat] = got_rows[lat].astype(F32)
        for row in range(MAIN):
            flat[pl.ds(row, 64, stride=SLOTS), :] = rows[lat, pl.ds(row, 64, stride=16), :]
        for i in range(SLOTS - MAIN):
            thirds = [
                pltpu.roll(
                    rows[lat, pl.ds(3 * i + th, 64, stride=16), :], (32 + 32 * th) % 128, 1
                )
                for th in range(3)
            ]
            flat[pl.ds(MAIN + i, 64, stride=SLOTS), :] = jnp.where(
                lane < 32, thirds[0], jnp.where(lane < 64, thirds[1], thirds[2])
            )
        for start in range(0, COLS, 128):
            gathered[:, start : start + 128] = (
                flat[start : start + 128, :].T[0:96].astype(BF16)
            )
        total = lax.dot_general(
            gathered[...], hot[...], (((1,), (1,)), ((), ())), preferred_element_type=F32
        )
        for k in range(2):
            modes[:, k * MPAD : (k + 1) * MPAD] = total[k * CDEV : k * CDEV + CDEV].astype(BF16)
        for strip in range(6):
            spatial = jnp.dot(
                modes[...],
                inverse_ref[:, strip * 256 : strip * 256 + 256],
                preferred_element_type=F32,
            )
            for block in (2 * strip, 2 * strip + 1):
                lanes = slice(block * 128, block * 128 + 128)
                if block < 11:
                    old = x_ref[lat, :, lanes].astype(F32)
                else:
                    old = jnp.concatenate(
                        [x_ref[lat, :, 1408:1440], jnp.zeros((CDEV, 96), BF16)], axis=1
                    ).astype(F32)
                at = (block % 2) * 128
                new = (old + spatial[:, at : at + 128]).astype(BF16)
                for part, place in places(lat, block):
                    updated[lat, part, :, place * 128 : place * 128 + 128] = new
        send_chan(updated, whole, 0, lat)
        if lat == 0:
            prepare_coef()
        else:
            mix(lat - 1)
    mix(LDEV - 1)
    for lat in range(LDEV):
        wait_chan(mixed, final, chan_recv, 1, lat)
        wait_space(out_rows, in_rows, send_sem, 0, lat)
        wait_space(back_rows, got_rows, send_sem, 1, lat)
        wait_chan(updated, whole, chan_send, 0, lat)
        wait_chan(mixed, final, chan_send, 1, lat)
    wait_coef(3, coef_send.at[0])
    wait_coef(4, coef_send.at[1])


def unpack_kernel(final_ref, out_ref):
    for lat in range(LDEV):
        for block in range(12):
            part, place = places(lat, block)[0]
            width = 128 if block < 11 else 32
            out_ref[lat, :, block * 128 : block * 128 + width] = final_ref[
                lat, part, :, place * 128 : place * 128 + width
            ]


def shards(state_field, slot_wave, spectral_filter, kan_coef):
    forward, inverse, weights, xrow, first, steps = make_tables()
    x = jnp.transpose(state_field, (1, 0, 2))
    cols = slot_wave.reshape(1, COLS)
    message = pltpu.VMEM((LDEV, SPACES * 16, 128), BF16)
    part = pltpu.VMEM((LDEV, CHANS, CDEV, PART), BF16)
    final = pl.pallas_call(
        block_kernel,
        out_shape=jax.ShapeDtypeStruct((LDEV, CHANS, CDEV, PART), BF16),
        in_specs=[HBM] * 5 + [SMEM] * 3 + [VMEM] * 3,
        out_specs=VMEM,
        scratch_shapes=[
            pltpu.VMEM((LDEV, CDEV, NLON), BF16),
            pltpu.VMEM((2, NLON, MPAD), BF16),
            pltpu.VMEM((2 * MPAD, NPAD), BF16),
            pltpu.VMEM((SLOTS, 2, CDEV, LMAX), BF16),
            pltpu.VMEM((2, CHANS // 2, BASIS, CDEV, 384), BF16),
            pltpu.SemaphoreType.DMA((5,)),
            pltpu.SemaphoreType.DMA((2, LDEV)),
            pltpu.SemaphoreType.DMA((2, LDEV)),
            pltpu.SemaphoreType.DMA((2, LDEV)),
            pltpu.SemaphoreType.DMA((2, LDEV)),
            pltpu.SemaphoreType.DMA((2,)),
            pltpu.SemaphoreType.DMA((2,)),
            pltpu.VMEM((MPAD, COLS), BF16),
            pltpu.VMEM((96, MPAD), BF16),
            pltpu.VMEM((96, COLS), F32),
            pltpu.VMEM((COLS, 128), F32),
            pltpu.VMEM((LDEV, SPACES * 16, 128), F32),
            message,
            message,
            pltpu.VMEM((DEG_SLOTS, 128), jnp.int32),
            pltpu.VMEM((DEG_SLOTS, 256), F32),
            pltpu.VMEM((2, CHUNK * DEG_SLOTS, 128), F32),
            pltpu.VMEM((SLOTS, LMAX, 256), BF16),
            pltpu.VMEM((SLOTS, 96, 256), BF16),
            pltpu.VMEM((SLOTS, 96, 256), F32),
            message,
            message,
            pltpu.VMEM((384, 5 * 384), BF16),
            pltpu.VMEM((384, 128), F32),
            pltpu.VMEM((96, COLS), BF16),
            pltpu.VMEM((CDEV, 2 * MPAD), BF16),
            pltpu.VMEM((5 * 384, PART), BF16),
            part,
            part,
            part,
        ],
        compiler_params=pltpu.CompilerParams(
            collective_id=0, has_side_effects=True, vmem_limit_bytes=60 * 1024 * 1024
        ),
        name="spectral_block",
    )(x, forward, inverse, spectral_filter, kan_coef, slot_wave, weights, steps, cols, xrow, first)
    out = pl.pallas_call(
        unpack_kernel,
        out_shape=jax.ShapeDtypeStruct((LDEV, CDEV, NLON), BF16),
        in_specs=[VMEM],
        out_specs=VMEM,
        name="unpack",
    )(final)
    return jnp.transpose(out, (1, 0, 2))


def solution(mesh):
    in_specs = (
        P("chan", "space", None),
        P(),
        P("space", None, "chan", None),
        P(None, "chan", None),
    )
    out_specs = P("chan", "space", None)
    return jax.shard_map(shards, mesh=mesh, in_specs=in_specs, out_specs=out_specs, check_vma=False)
```

```python
import math

import jax
import jax.numpy as jnp
import ml_dtypes
import numpy as np
from jax import lax
from jax.experimental import pallas as pl
from jax.experimental.pallas import tpu as pltpu
from jax.sharding import PartitionSpec as P

NLON = 1440
MMAX = 720
LMAX = 720
BASIS = 6
MPAD = 768
NPAD = 1536
SLOTS = 18
MAIN = 16
SPACES = 64
CHANS = 8
CDEV = 48
LDEV = 3
LAT = 192
ROWS = 48
COLS = 1152
PART = 256
DEG_SLOTS = 24
CHUNK = 240
F32 = jnp.float32
BF16 = jnp.bfloat16

VMEM = pl.BlockSpec(memory_space=pltpu.VMEM)
SMEM = pl.BlockSpec(memory_space=pltpu.SMEM)
HBM = pl.BlockSpec(memory_space=pl.ANY)
MESH = pl.DeviceIdType.MESH


def make_tables():
    m = np.arange(MMAX)[:, None]
    n = np.arange(NLON)[None, :]
    angle = (m * n % NLON) * (2.0 * np.pi / NLON)
    cos, sin = np.cos(angle), np.sin(angle)
    forward = np.zeros((2, NLON, MPAD))
    forward[0, :, :MMAX] = cos.T / NLON
    forward[1, :, :MMAX] = -sin.T / NLON
    factor = np.where(m == 0, 1.0, 2.0)
    inverse = np.zeros((2 * MPAD, NPAD))
    inverse[:MMAX, :NLON] = factor * cos
    inverse[MPAD : MPAD + MMAX, :NLON] = -factor * sin
    lat = np.arange(LAT)
    colat = 0.5 * np.pi + (lat + 0.5 - 0.5 * LAT) * (np.pi / LMAX)
    weights = (2.0 * np.pi * np.pi / LMAX * np.sin(colat)).astype(np.float32)
    order = (3 * np.arange(SPACES)[None, :] + np.arange(LDEV)[:, None]).reshape(-1)
    xrow = np.zeros((8, 256), np.float32)
    xrow[:, :LAT] = np.cos(colat)[order]
    first = np.zeros((MMAX + 8, 256), np.float32)
    for wave in range(MMAX):
        base = 0.5 * (
            math.log((2.0 * wave + 1.0) / (4.0 * math.pi))
            + math.lgamma(wave + 0.5)
            - math.lgamma(wave + 1.0)
            - 0.5 * math.log(math.pi)
        )
        first[wave, :LAT] = np.exp(base + wave * np.log(np.sin(colat)))[order]
    degree = np.arange(LMAX, dtype=np.float64)
    root = np.sqrt(np.maximum(4.0 * degree * degree - 1.0, 1.0))
    steps = np.stack([degree * degree, root, 1.0 / root]).astype(np.float32)
    return (
        forward.astype(ml_dtypes.bfloat16),
        inverse.astype(ml_dtypes.bfloat16),
        weights,
        xrow,
        first,
        steps,
    )


def one_hot(cols_row, start, size):
    waves = lax.broadcasted_iota(jnp.int32, (MPAD, size), 0)
    return jnp.where(waves == cols_row[0:1, start : start + size], 1.0, 0.0).astype(BF16)


ORDER = sorted(
    ((k // 8, k % 8) for k in range(1, SPACES)),
    key=lambda step: -min(step[0], 8 - step[0]) - min(step[1], 8 - step[1]),
)


def places(lat, block):
    chip, inner = block // 3, block % 3
    if lat == 1:
        return [[(2 * chip, 0), (2 * chip, 1)], [(2 * chip + 1, 0)], [(2 * chip + 1, 1)]][inner]
    return [[(2 * chip, 0)], [(2 * chip, 1)], [(2 * chip + 1, 0), (2 * chip + 1, 1)]][inner]


def block_kernel(
    x_hbm,
    forward_hbm,
    inverse_hbm,
    gain_hbm,
    coef_hbm,
    wave_ref,
    weight_ref,
    steps_ref,
    cols_ref,
    xrow_ref,
    first_ref,
    final,
    x_ref,
    forward_ref,
    inverse_ref,
    gain_ref,
    coefs,
    load_sem,
    send_sem,
    recv_sem,
    chan_send,
    chan_recv,
    coef_send,
    coef_recv,
    hot,
    zonal,
    packed,
    flat,
    rows,
    out_rows,
    in_rows,
    order_ref,
    start_ref,
    grown,
    legendre,
    spread,
    made,
    back_rows,
    got_rows,
    coef_ref,
    bias_ref,
    gathered,
    modes,
    basis,
    updated,
    whole,
    mixed,
):
    here = lax.axis_index("space")
    group = lax.axis_index("chan")
    here_y, here_z = here // 8, here % 8
    chip, core = group // 2, group % 2
    sibling = chip * 2 + 1 - core

    loads = [
        pltpu.make_async_copy(source, target, load_sem.at[i])
        for i, (source, target) in enumerate(
            (
                (x_hbm, x_ref),
                (forward_hbm, forward_ref),
                (inverse_hbm, inverse_ref),
                (gain_hbm, gain_ref),
                (coef_hbm, coefs.at[core, chip]),
            )
        )
    ]
    load_x, load_forward, load_inverse, load_gain, load_coef = loads
    load_x.start()
    load_forward.start()

    barrier = pltpu.get_barrier_semaphore()

    for oy, oz in ORDER:
        peer = lax.rem(here_y + oy, 8) * 8 + lax.rem(here_z + oz, 8)
        pl.semaphore_signal(barrier, inc=1, device_id={"space": peer}, device_id_type=MESH)
    for k in range(1, CHANS):
        peer = lax.rem(group + k, CHANS)
        pl.semaphore_signal(barrier, inc=1, device_id={"chan": peer}, device_id_type=MESH)

    def send_space(source, target, step, lat):
        for oy, oz in ORDER:
            peer = lax.rem(here_y + oy, 8) * 8 + lax.rem(here_z + oz, 8)
            pltpu.make_async_remote_copy(
                src_ref=source.at[lat, pl.ds(pl.multiple_of(peer * 16, 16), 16)],
                dst_ref=target.at[lat, pl.ds(pl.multiple_of(here * 16, 16), 16)],
                send_sem=send_sem.at[step, lat],
                recv_sem=recv_sem.at[step, lat],
                device_id={"space": peer},
                device_id_type=MESH,
            ).start()
        own = pl.ds(pl.multiple_of(here * 16, 16), 16)
        target[lat, own, :] = source[lat, own, :]

    def wait_space(source, target, sem, step, lat):
        most = pl.ds(0, (SPACES - 1) * 16)
        pltpu.make_async_copy(
            source.at[lat, most], target.at[lat, most], sem.at[step, lat]
        ).wait()

    def send_chan(source, target, step, lat):
        for offset in (4, 3, 5, 2, 6, 7, 1):
            peer = lax.rem(group + offset, CHANS)
            pltpu.make_async_remote_copy(
                src_ref=source.at[lat, peer],
                dst_ref=target.at[lat, group],
                send_sem=chan_send.at[step, lat],
                recv_sem=chan_recv.at[step, lat],
                device_id={"chan": peer},
                device_id_type=MESH,
            ).start()
        target[lat, group] = source[lat, group]

    def wait_chan(source, target, sem, step, lat):
        most = pl.ds(0, CHANS - 1)
        pltpu.make_async_copy(
            source.at[lat, most], target.at[lat, most], sem.at[step, lat]
        ).wait()

    def send_coef(k, carry):
        pltpu.make_async_remote_copy(
            src_ref=coefs.at[core, chip],
            dst_ref=coefs.at[core, chip],
            send_sem=coef_send.at[0],
            recv_sem=coef_recv.at[0],
            device_id={"chan": lax.rem(group + 2 * k, CHANS)},
            device_id_type=MESH,
        ).start()
        return carry

    def wait_coef(count, sem):
        most = pl.ds(0, count)
        pltpu.make_async_copy(coefs.at[0, most], coefs.at[0, most], sem).wait()

    lane = lax.broadcasted_iota(jnp.int32, (64, 128), 1)
    tail_lane = lane >= 96
    flat[...] = jnp.zeros_like(flat)
    cols = cols_ref[...]
    for start in range(0, COLS, 128):
        hot[:, start : start + 128] = one_hot(cols, start, 128)
    load_x.wait()
    load_forward.wait()
    for load in (load_coef, load_gain, load_inverse):
        load.start()
    for lat in range(LDEV):
        weight = weight_ref[here * LDEV + lat]
        for k in range(2):
            part = jnp.dot(x_ref[lat], forward_ref[k], preferred_element_type=F32)
            zonal[k * CDEV : k * CDEV + CDEV, :] = (part * weight).astype(BF16)
        packed[...] = jnp.dot(zonal[...], hot[...], preferred_element_type=F32)
        for start in range(0, COLS, 128):
            flat[start : start + 128, 0:96] = packed[:, start : start + 128].T
        for row in range(MAIN):
            line = flat[pl.ds(row, 64, stride=SLOTS), :]
            if row < 6:
                last = flat[pl.ds(MAIN + row // 3, 64, stride=SLOTS), :]
                line = jnp.where(tail_lane, pltpu.roll(last, 96 - 32 * (row % 3), 1), line)
            rows[lat, pl.ds(row, 64, stride=16), :] = line
        out_rows[lat] = rows[lat].astype(BF16)
        if lat == 0:
            pl.semaphore_wait(barrier, SPACES - 1 + CHANS - 1)
        send_space(out_rows, in_rows, 0, lat)
        if lat == 0:
            load_coef.wait()
            lax.fori_loop(1, 4, send_coef, 0)


    for slot in range(DEG_SLOTS):
        wave = wave_ref[here * SLOTS + slot] if slot < SLOTS else MMAX
        order_ref[slot : slot + 1, :] = jnp.full((1, 128), wave, jnp.int32)
        start_ref[slot : slot + 1, :] = first_ref[pl.ds(wave, 1), :]
    order = order_ref[...]
    square = order.astype(F32) * order.astype(F32)
    first_a, first_b = start_ref[:, 0:128], start_ref[:, 128:256]
    x_a = jnp.broadcast_to(xrow_ref[0:1, 0:128], (DEG_SLOTS, 128))
    x_b = jnp.broadcast_to(xrow_ref[0:1, 128:256], (DEG_SLOTS, 128))
    zero = jnp.zeros((DEG_SLOTS, 128), F32)
    state = (zero, zero, zero, zero, zero)
    for chunk in range(LMAX // CHUNK):

        def advance(block, carry, chunk=chunk):
            now_a, before_a, now_b, before_b, falling = carry
            for offset in range(8):
                at = block * 8 + offset
                degree = chunk * CHUNK + at
                gap = steps_ref[0, degree] - square
                inverse_root = lax.rsqrt(jnp.maximum(gap, 1.0))
                rising = steps_ref[1, degree] * inverse_root
                starts = order == degree
                next_a = jnp.where(starts, first_a, rising * (x_a * now_a - falling * before_a))
                next_b = jnp.where(starts, first_b, rising * (x_b * now_b - falling * before_b))
                falling = gap * inverse_root * steps_ref[2, degree]
                now_a, before_a, now_b, before_b = next_a, now_a, next_b, now_b
                grown[0, pl.ds(at * DEG_SLOTS, DEG_SLOTS), :] = next_a
                grown[1, pl.ds(at * DEG_SLOTS, DEG_SLOTS), :] = next_b
            return now_a, before_a, now_b, before_b, falling

        state = lax.fori_loop(0, CHUNK // 8, advance, state)

        def lay_out(slot, carry, chunk=chunk):
            for half in range(2):
                legendre[
                    slot, chunk * CHUNK : chunk * CHUNK + CHUNK, half * 128 : half * 128 + 128
                ] = grown[half, pl.ds(slot, CHUNK, stride=DEG_SLOTS), :].astype(BF16)
            return carry

        lax.fori_loop(0, SLOTS, lay_out, 0)

    for lats in ((0, 1), (2,)):
        for lat in lats:
            wait_space(out_rows, in_rows, recv_sem, 0, lat)
            rows[lat] = in_rows[lat].astype(F32)
        lanes = slice(lats[0] * 64, lats[0] * 64 + 128)
        for row in range(MAIN):
            stack = [rows[lat, pl.ds(row, 64, stride=16), :] for lat in lats]
            if len(lats) == 1:
                stack.append(jnp.zeros((64, 128), F32))
            turned = jnp.concatenate(stack, axis=0).T.astype(BF16)
            spread[row, :, lanes] = turned[0:96]
            if row < 6:
                at = 32 * (row % 3)
                spread[MAIN + row // 3, at : at + 32, lanes] = turned[96:128]
    load_gain.wait()

    def filter_slots(step, carry):
        slots = [step * 9 + i for i in range(9)]
        spectra = [
            lax.dot_general(
                spread[slot], legendre[slot], (((1,), (1,)), ((), ())), preferred_element_type=F32
            )
            for slot in slots
        ]
        for slot, spectrum in zip(slots, spectra):
            real, imag = spectrum[0:CDEV], spectrum[CDEV:96]
            gain_real = gain_ref[slot, 0].astype(F32)
            gain_imag = gain_ref[slot, 1].astype(F32)
            filtered = jnp.concatenate(
                [gain_real * real - gain_imag * imag, gain_real * imag + gain_imag * real], axis=0
            ).astype(BF16)
            made[slot] = jnp.dot(filtered, legendre[slot], preferred_element_type=F32)
        return carry

    lax.fori_loop(0, SLOTS // 9, filter_slots, 0)
    for lats in ((0, 1), (2,)):
        lanes = slice(lats[0] * 64, lats[0] * 64 + 128)
        for row in range(MAIN):
            extra = jnp.zeros((32, 128), F32)
            if row < 6:
                at = 32 * (row % 3)
                extra = made[MAIN + row // 3, at : at + 32, lanes]
            turned = jnp.concatenate([made[row, :, lanes], extra], axis=0).T
            for i, lat in enumerate(lats):
                rows[lat, pl.ds(row, 64, stride=16), :] = turned[i * 64 : i * 64 + 64]
        for lat in lats:
            back_rows[lat] = rows[lat].astype(BF16)
            send_space(back_rows, got_rows, 1, lat)

    wait_coef(3, coef_recv.at[0])
    pltpu.make_async_remote_copy(
        src_ref=coefs.at[core],
        dst_ref=coefs.at[core],
        send_sem=coef_send.at[1],
        recv_sem=coef_recv.at[1],
        device_id={"chan": sibling},
        device_id_type=MESH,
    ).start()

    load_inverse.wait()

    def mix(lat):
        wait_chan(updated, whole, chan_recv, 0, lat)
        u = whole[lat].reshape(384, PART).astype(F32)
        t = jnp.tanh(u)
        base = 0.5 * u * (1.0 + jnp.tanh(0.5 * u))
        second = 2.0 * t * t - 1.0
        third = 2.0 * t * second - t
        fourth = 2.0 * t * third - second
        for k, piece in enumerate((base, t, second, third, fourth)):
            basis[k * 384 : k * 384 + 384, :] = piece.astype(BF16)
        for half in range(2):
            total = jnp.dot(
                coef_ref[half * 192 : half * 192 + 192, :], basis[...], preferred_element_type=F32
            )
            bias = bias_ref[half * 192 : half * 192 + 192, 0:1]
            mixed[lat, half * 4 : half * 4 + 4] = (
                (total + bias).astype(BF16).reshape(4, CDEV, PART)
            )
        send_chan(mixed, final, 1, lat)

    def prepare_coef():
        wait_coef(4, coef_recv.at[1])
        for k in range(BASIS):
            turned = jnp.concatenate(
                [coefs[g % 2, g // 2, k] for g in range(CHANS)], axis=0
            ).astype(F32).T
            if k == 1:
                bias_ref[...] = jnp.broadcast_to(
                    jnp.sum(turned, axis=1, keepdims=True), bias_ref.shape
                )
            else:
                at = (k if k == 0 else k - 1) * 384
                coef_ref[:, at : at + 384] = turned.astype(BF16)

    for lat in range(LDEV):
        wait_space(back_rows, got_rows, recv_sem, 1, lat)
        rows[lat] = got_rows[lat].astype(F32)
        for row in range(MAIN):
            flat[pl.ds(row, 64, stride=SLOTS), :] = rows[lat, pl.ds(row, 64, stride=16), :]
        for i in range(SLOTS - MAIN):
            thirds = [
                pltpu.roll(
                    rows[lat, pl.ds(3 * i + th, 64, stride=16), :], (32 + 32 * th) % 128, 1
                )
                for th in range(3)
            ]
            flat[pl.ds(MAIN + i, 64, stride=SLOTS), :] = jnp.where(
                lane < 32, thirds[0], jnp.where(lane < 64, thirds[1], thirds[2])
            )
        for start in range(0, COLS, 128):
            gathered[:, start : start + 128] = (
                flat[start : start + 128, :].T[0:96].astype(BF16)
            )
        total = lax.dot_general(
            gathered[...], hot[...], (((1,), (1,)), ((), ())), preferred_element_type=F32
        )
        for k in range(2):
            modes[:, k * MPAD : (k + 1) * MPAD] = total[k * CDEV : k * CDEV + CDEV].astype(BF16)
        for strip in range(6):
            spatial = jnp.dot(
                modes[...],
                inverse_ref[:, strip * 256 : strip * 256 + 256],
                preferred_element_type=F32,
            )
            for block in (2 * strip, 2 * strip + 1):
                lanes = slice(block * 128, block * 128 + 128)
                if block < 11:
                    old = x_ref[lat, :, lanes].astype(F32)
                else:
                    old = jnp.concatenate(
                        [x_ref[lat, :, 1408:1440], jnp.zeros((CDEV, 96), BF16)], axis=1
                    ).astype(F32)
                at = (block % 2) * 128
                new = (old + spatial[:, at : at + 128]).astype(BF16)
                for part, place in places(lat, block):
                    updated[lat, part, :, place * 128 : place * 128 + 128] = new
        send_chan(updated, whole, 0, lat)
        if lat == 0:
            prepare_coef()
        else:
            mix(lat - 1)
    mix(LDEV - 1)
    for lat in range(LDEV):
        wait_chan(mixed, final, chan_recv, 1, lat)
        wait_space(out_rows, in_rows, send_sem, 0, lat)
        wait_space(back_rows, got_rows, send_sem, 1, lat)
        wait_chan(updated, whole, chan_send, 0, lat)
        wait_chan(mixed, final, chan_send, 1, lat)
    wait_coef(3, coef_send.at[0])
    wait_coef(4, coef_send.at[1])


def unpack_kernel(final_ref, out_ref):
    for lat in range(LDEV):
        for block in range(12):
            part, place = places(lat, block)[0]
            width = 128 if block < 11 else 32
            out_ref[lat, :, block * 128 : block * 128 + width] = final_ref[
                lat, part, :, place * 128 : place * 128 + width
            ]


def shards(state_field, slot_wave, spectral_filter, kan_coef):
    forward, inverse, weights, xrow, first, steps = make_tables()
    x = jnp.transpose(state_field, (1, 0, 2))
    cols = slot_wave.reshape(1, COLS)
    message = pltpu.VMEM((LDEV, SPACES * 16, 128), BF16)
    part = pltpu.VMEM((LDEV, CHANS, CDEV, PART), BF16)
    final = pl.pallas_call(
        block_kernel,
        out_shape=jax.ShapeDtypeStruct((LDEV, CHANS, CDEV, PART), BF16),
        in_specs=[HBM] * 5 + [SMEM] * 3 + [VMEM] * 3,
        out_specs=VMEM,
        scratch_shapes=[
            pltpu.VMEM((LDEV, CDEV, NLON), BF16),
            pltpu.VMEM((2, NLON, MPAD), BF16),
            pltpu.VMEM((2 * MPAD, NPAD), BF16),
            pltpu.VMEM((SLOTS, 2, CDEV, LMAX), BF16),
            pltpu.VMEM((2, CHANS // 2, BASIS, CDEV, 384), BF16),
            pltpu.SemaphoreType.DMA((5,)),
            pltpu.SemaphoreType.DMA((2, LDEV)),
            pltpu.SemaphoreType.DMA((2, LDEV)),
            pltpu.SemaphoreType.DMA((2, LDEV)),
            pltpu.SemaphoreType.DMA((2, LDEV)),
            pltpu.SemaphoreType.DMA((2,)),
            pltpu.SemaphoreType.DMA((2,)),
            pltpu.VMEM((MPAD, COLS), BF16),
            pltpu.VMEM((96, MPAD), BF16),
            pltpu.VMEM((96, COLS), F32),
            pltpu.VMEM((COLS, 128), F32),
            pltpu.VMEM((LDEV, SPACES * 16, 128), F32),
            message,
            message,
            pltpu.VMEM((DEG_SLOTS, 128), jnp.int32),
            pltpu.VMEM((DEG_SLOTS, 256), F32),
            pltpu.VMEM((2, CHUNK * DEG_SLOTS, 128), F32),
            pltpu.VMEM((SLOTS, LMAX, 256), BF16),
            pltpu.VMEM((SLOTS, 96, 256), BF16),
            pltpu.VMEM((SLOTS, 96, 256), F32),
            message,
            message,
            pltpu.VMEM((384, 5 * 384), BF16),
            pltpu.VMEM((384, 128), F32),
            pltpu.VMEM((96, COLS), BF16),
            pltpu.VMEM((CDEV, 2 * MPAD), BF16),
            pltpu.VMEM((5 * 384, PART), BF16),
            part,
            part,
            part,
        ],
        compiler_params=pltpu.CompilerParams(
            collective_id=0, has_side_effects=True, vmem_limit_bytes=60 * 1024 * 1024
        ),
        name="spectral_block",
    )(x, forward, inverse, spectral_filter, kan_coef, slot_wave, weights, steps, cols, xrow, first)
    out = pl.pallas_call(
        unpack_kernel,
        out_shape=jax.ShapeDtypeStruct((LDEV, CDEV, NLON), BF16),
        in_specs=[VMEM],
        out_specs=VMEM,
        name="unpack",
    )(final)
    return jnp.transpose(out, (1, 0, 2))


def solution(mesh):
    in_specs = (
        P("chan", "space", None),
        P(),
        P("space", None, "chan", None),
        P(None, "chan", None),
    )
    out_specs = P("chan", "space", None)
    return jax.shard_map(shards, mesh=mesh, in_specs=in_specs, out_specs=out_specs, check_vma=False)
```

```python
import math

import jax
import jax.numpy as jnp
import ml_dtypes
import numpy as np
from jax import lax
from jax.experimental import pallas as pl
from jax.experimental.pallas import tpu as pltpu
from jax.sharding import PartitionSpec as P

NLON = 1440
MMAX = 720
LMAX = 720
BASIS = 6
MPAD = 768
NPAD = 1536
SLOTS = 18
MAIN = 16
SPACES = 64
CHANS = 8
CDEV = 48
LDEV = 3
LAT = 192
ROWS = 48
COLS = 1152
PART = 256
DEG_SLOTS = 24
CHUNK = 240
F32 = jnp.float32
BF16 = jnp.bfloat16

VMEM = pl.BlockSpec(memory_space=pltpu.VMEM)
SMEM = pl.BlockSpec(memory_space=pltpu.SMEM)
HBM = pl.BlockSpec(memory_space=pl.ANY)
MESH = pl.DeviceIdType.MESH


def make_tables():
    m = np.arange(MMAX)[:, None]
    n = np.arange(NLON)[None, :]
    angle = (m * n % NLON) * (2.0 * np.pi / NLON)
    cos, sin = np.cos(angle), np.sin(angle)
    forward = np.zeros((2, NLON, MPAD))
    forward[0, :, :MMAX] = cos.T / NLON
    forward[1, :, :MMAX] = -sin.T / NLON
    factor = np.where(m == 0, 1.0, 2.0)
    inverse = np.zeros((2 * MPAD, NPAD))
    inverse[:MMAX, :NLON] = factor * cos
    inverse[MPAD : MPAD + MMAX, :NLON] = -factor * sin
    lat = np.arange(LAT)
    colat = 0.5 * np.pi + (lat + 0.5 - 0.5 * LAT) * (np.pi / LMAX)
    weights = (2.0 * np.pi * np.pi / LMAX * np.sin(colat)).astype(np.float32)
    order = (3 * np.arange(SPACES)[None, :] + np.arange(LDEV)[:, None]).reshape(-1)
    xrow = np.zeros((8, 256), np.float32)
    xrow[:, :LAT] = np.cos(colat)[order]
    first = np.zeros((MMAX + 8, 256), np.float32)
    for wave in range(MMAX):
        base = 0.5 * (
            math.log((2.0 * wave + 1.0) / (4.0 * math.pi))
            + math.lgamma(wave + 0.5)
            - math.lgamma(wave + 1.0)
            - 0.5 * math.log(math.pi)
        )
        first[wave, :LAT] = np.exp(base + wave * np.log(np.sin(colat)))[order]
    degree = np.arange(LMAX, dtype=np.float64)
    root = np.sqrt(np.maximum(4.0 * degree * degree - 1.0, 1.0))
    steps = np.stack([degree * degree, root, 1.0 / root]).astype(np.float32)
    return (
        forward.astype(ml_dtypes.bfloat16),
        inverse.astype(ml_dtypes.bfloat16),
        weights,
        xrow,
        first,
        steps,
    )


def one_hot(cols_row, start, size):
    waves = lax.broadcasted_iota(jnp.int32, (MPAD, size), 0)
    return jnp.where(waves == cols_row[0:1, start : start + size], 1.0, 0.0).astype(BF16)


ORDER = sorted(
    ((k // 8, k % 8) for k in range(1, SPACES)),
    key=lambda step: -min(step[0], 8 - step[0]) - min(step[1], 8 - step[1]),
)


def places(lat, block):
    chip, inner = block // 3, block % 3
    if lat == 1:
        return [[(2 * chip, 0), (2 * chip, 1)], [(2 * chip + 1, 0)], [(2 * chip + 1, 1)]][inner]
    return [[(2 * chip, 0)], [(2 * chip, 1)], [(2 * chip + 1, 0), (2 * chip + 1, 1)]][inner]


def block_kernel(
    x_hbm,
    forward_hbm,
    inverse_hbm,
    gain_hbm,
    coef_hbm,
    wave_ref,
    weight_ref,
    steps_ref,
    cols_ref,
    xrow_ref,
    first_ref,
    final,
    x_ref,
    forward_ref,
    inverse_ref,
    gain_ref,
    coefs,
    load_sem,
    send_sem,
    recv_sem,
    chan_send,
    chan_recv,
    coef_send,
    coef_recv,
    hot,
    zonal,
    packed,
    flat,
    rows,
    out_rows,
    in_rows,
    order_ref,
    start_ref,
    grown,
    legendre,
    spread,
    made,
    back_rows,
    got_rows,
    coef_ref,
    bias_ref,
    gathered,
    modes,
    basis,
    updated,
    whole,
    mixed,
):
    here = lax.axis_index("space")
    group = lax.axis_index("chan")
    here_y, here_z = here // 8, here % 8
    chip, core = group // 2, group % 2
    sibling = chip * 2 + 1 - core

    loads = [
        pltpu.make_async_copy(source, target, load_sem.at[i])
        for i, (source, target) in enumerate(
            (
                (x_hbm, x_ref),
                (forward_hbm.at[0], forward_ref.at[0]),
                (forward_hbm.at[1], forward_ref.at[1]),
                (inverse_hbm, inverse_ref),
                (gain_hbm, gain_ref),
                (coef_hbm, coefs.at[core, chip]),
            )
        )
    ]
    load_x, load_real, load_imag, load_inverse, load_gain, load_coef = loads
    load_x.start()
    load_real.start()
    load_imag.start()

    barrier = pltpu.get_barrier_semaphore()

    for oy, oz in ORDER:
        peer = lax.rem(here_y + oy, 8) * 8 + lax.rem(here_z + oz, 8)
        pl.semaphore_signal(barrier, inc=1, device_id={"space": peer}, device_id_type=MESH)
    for k in range(1, CHANS):
        peer = lax.rem(group + k, CHANS)
        pl.semaphore_signal(barrier, inc=1, device_id={"chan": peer}, device_id_type=MESH)

    def send_space(source, target, step, lat):
        for oy, oz in ORDER:
            peer = lax.rem(here_y + oy, 8) * 8 + lax.rem(here_z + oz, 8)
            pltpu.make_async_remote_copy(
                src_ref=source.at[lat, pl.ds(pl.multiple_of(peer * 16, 16), 16)],
                dst_ref=target.at[lat, pl.ds(pl.multiple_of(here * 16, 16), 16)],
                send_sem=send_sem.at[step, lat],
                recv_sem=recv_sem.at[step, lat],
                device_id={"space": peer},
                device_id_type=MESH,
            ).start()
        own = pl.ds(pl.multiple_of(here * 16, 16), 16)
        target[lat, own, :] = source[lat, own, :]

    def wait_space(source, target, sem, step, lat):
        most = pl.ds(0, (SPACES - 1) * 16)
        pltpu.make_async_copy(
            source.at[lat, most], target.at[lat, most], sem.at[step, lat]
        ).wait()

    def send_chan(source, target, step, lat):
        for offset in (4, 3, 5, 2, 6, 7, 1):
            peer = lax.rem(group + offset, CHANS)
            pltpu.make_async_remote_copy(
                src_ref=source.at[lat, peer],
                dst_ref=target.at[lat, group],
                send_sem=chan_send.at[step, lat],
                recv_sem=chan_recv.at[step, lat],
                device_id={"chan": peer},
                device_id_type=MESH,
            ).start()
        target[lat, group] = source[lat, group]

    def wait_chan(source, target, sem, step, lat):
        most = pl.ds(0, CHANS - 1)
        pltpu.make_async_copy(
            source.at[lat, most], target.at[lat, most], sem.at[step, lat]
        ).wait()

    def send_coef(k, carry):
        pltpu.make_async_remote_copy(
            src_ref=coefs.at[core, chip],
            dst_ref=coefs.at[core, chip],
            send_sem=coef_send.at[0],
            recv_sem=coef_recv.at[0],
            device_id={"chan": lax.rem(group + 2 * k, CHANS)},
            device_id_type=MESH,
        ).start()
        return carry

    def wait_coef(count, sem):
        most = pl.ds(0, count)
        pltpu.make_async_copy(coefs.at[0, most], coefs.at[0, most], sem).wait()

    lane = lax.broadcasted_iota(jnp.int32, (64, 128), 1)
    tail_lane = lane >= 96
    flat[...] = jnp.zeros_like(flat)
    cols = cols_ref[...]
    for start in range(0, COLS, 128):
        hot[:, start : start + 128] = one_hot(cols, start, 128)
    load_x.wait()
    for lat in range(LDEV):
        weight = weight_ref[here * LDEV + lat]
        for k in range(2):
            if lat == 0:
                (load_real, load_imag)[k].wait()
            part = jnp.dot(x_ref[lat], forward_ref[k], preferred_element_type=F32)
            zonal[k * CDEV : k * CDEV + CDEV, :] = (part * weight).astype(BF16)
        if lat == 0:
            for load in (load_coef, load_gain, load_inverse):
                load.start()
        packed[...] = jnp.dot(zonal[...], hot[...], preferred_element_type=F32)
        for start in range(0, COLS, 128):
            flat[start : start + 128, 0:96] = packed[:, start : start + 128].T
        for row in range(MAIN):
            line = flat[pl.ds(row, 64, stride=SLOTS), :]
            if row < 6:
                last = flat[pl.ds(MAIN + row // 3, 64, stride=SLOTS), :]
                line = jnp.where(tail_lane, pltpu.roll(last, 96 - 32 * (row % 3), 1), line)
            rows[lat, pl.ds(row, 64, stride=16), :] = line
        out_rows[lat] = rows[lat].astype(BF16)
        if lat == 0:
            pl.semaphore_wait(barrier, SPACES - 1 + CHANS - 1)
        send_space(out_rows, in_rows, 0, lat)
        if lat == 0:
            load_coef.wait()
            lax.fori_loop(1, 4, send_coef, 0)


    for slot in range(DEG_SLOTS):
        wave = wave_ref[here * SLOTS + slot] if slot < SLOTS else MMAX
        order_ref[slot : slot + 1, :] = jnp.full((1, 128), wave, jnp.int32)
        start_ref[slot : slot + 1, :] = first_ref[pl.ds(wave, 1), :]
    order = order_ref[...]
    square = order.astype(F32) * order.astype(F32)
    first_a, first_b = start_ref[:, 0:128], start_ref[:, 128:256]
    x_a = jnp.broadcast_to(xrow_ref[0:1, 0:128], (DEG_SLOTS, 128))
    x_b = jnp.broadcast_to(xrow_ref[0:1, 128:256], (DEG_SLOTS, 128))
    zero = jnp.zeros((DEG_SLOTS, 128), F32)
    state = (zero, zero, zero, zero, zero)
    for chunk in range(LMAX // CHUNK):

        def advance(block, carry, chunk=chunk):
            now_a, before_a, now_b, before_b, falling = carry
            for offset in range(8):
                at = block * 8 + offset
                degree = chunk * CHUNK + at
                gap = steps_ref[0, degree] - square
                inverse_root = lax.rsqrt(jnp.maximum(gap, 1.0))
                rising = steps_ref[1, degree] * inverse_root
                starts = order == degree
                next_a = jnp.where(starts, first_a, rising * (x_a * now_a - falling * before_a))
                next_b = jnp.where(starts, first_b, rising * (x_b * now_b - falling * before_b))
                falling = gap * inverse_root * steps_ref[2, degree]
                now_a, before_a, now_b, before_b = next_a, now_a, next_b, now_b
                grown[0, pl.ds(at * DEG_SLOTS, DEG_SLOTS), :] = next_a
                grown[1, pl.ds(at * DEG_SLOTS, DEG_SLOTS), :] = next_b
            return now_a, before_a, now_b, before_b, falling

        state = lax.fori_loop(0, CHUNK // 8, advance, state)

        def lay_out(slot, carry, chunk=chunk):
            for half in range(2):
                legendre[
                    slot, chunk * CHUNK : chunk * CHUNK + CHUNK, half * 128 : half * 128 + 128
                ] = grown[half, pl.ds(slot, CHUNK, stride=DEG_SLOTS), :].astype(BF16)
            return carry

        lax.fori_loop(0, SLOTS, lay_out, 0)

    for lats in ((0, 1), (2,)):
        for lat in lats:
            wait_space(out_rows, in_rows, recv_sem, 0, lat)
            rows[lat] = in_rows[lat].astype(F32)
        lanes = slice(lats[0] * 64, lats[0] * 64 + 128)
        for row in range(MAIN):
            stack = [rows[lat, pl.ds(row, 64, stride=16), :] for lat in lats]
            if len(lats) == 1:
                stack.append(jnp.zeros((64, 128), F32))
            turned = jnp.concatenate(stack, axis=0).T.astype(BF16)
            spread[row, :, lanes] = turned[0:96]
            if row < 6:
                at = 32 * (row % 3)
                spread[MAIN + row // 3, at : at + 32, lanes] = turned[96:128]
    load_gain.wait()

    def filter_slots(step, carry):
        slots = [step * 9 + i for i in range(9)]
        spectra = [
            lax.dot_general(
                spread[slot], legendre[slot], (((1,), (1,)), ((), ())), preferred_element_type=F32
            )
            for slot in slots
        ]
        for slot, spectrum in zip(slots, spectra):
            real, imag = spectrum[0:CDEV], spectrum[CDEV:96]
            gain_real = gain_ref[slot, 0].astype(F32)
            gain_imag = gain_ref[slot, 1].astype(F32)
            filtered = jnp.concatenate(
                [gain_real * real - gain_imag * imag, gain_real * imag + gain_imag * real], axis=0
            ).astype(BF16)
            made[slot] = jnp.dot(filtered, legendre[slot], preferred_element_type=F32)
        return carry

    lax.fori_loop(0, SLOTS // 9, filter_slots, 0)
    for lats in ((0, 1), (2,)):
        lanes = slice(lats[0] * 64, lats[0] * 64 + 128)
        for row in range(MAIN):
            extra = jnp.zeros((32, 128), F32)
            if row < 6:
                at = 32 * (row % 3)
                extra = made[MAIN + row // 3, at : at + 32, lanes]
            turned = jnp.concatenate([made[row, :, lanes], extra], axis=0).T
            for i, lat in enumerate(lats):
                rows[lat, pl.ds(row, 64, stride=16), :] = turned[i * 64 : i * 64 + 64]
        for lat in lats:
            back_rows[lat] = rows[lat].astype(BF16)
            send_space(back_rows, got_rows, 1, lat)

    wait_coef(3, coef_recv.at[0])
    pltpu.make_async_remote_copy(
        src_ref=coefs.at[core],
        dst_ref=coefs.at[core],
        send_sem=coef_send.at[1],
        recv_sem=coef_recv.at[1],
        device_id={"chan": sibling},
        device_id_type=MESH,
    ).start()

    load_inverse.wait()

    def mix(lat):
        wait_chan(updated, whole, chan_recv, 0, lat)
        u = whole[lat].reshape(384, PART).astype(F32)
        t = jnp.tanh(u)
        base = 0.5 * u * (1.0 + jnp.tanh(0.5 * u))
        second = 2.0 * t * t - 1.0
        third = 2.0 * t * second - t
        fourth = 2.0 * t * third - second
        for k, piece in enumerate((base, t, second, third, fourth)):
            basis[k * 384 : k * 384 + 384, :] = piece.astype(BF16)
        for half in range(2):
            total = jnp.dot(
                coef_ref[half * 192 : half * 192 + 192, :], basis[...], preferred_element_type=F32
            )
            bias = bias_ref[half * 192 : half * 192 + 192, 0:1]
            mixed[lat, half * 4 : half * 4 + 4] = (
                (total + bias).astype(BF16).reshape(4, CDEV, PART)
            )
        send_chan(mixed, final, 1, lat)

    def prepare_coef():
        wait_coef(4, coef_recv.at[1])
        for k in range(BASIS):
            turned = jnp.concatenate(
                [coefs[g % 2, g // 2, k] for g in range(CHANS)], axis=0
            ).astype(F32).T
            if k == 1:
                bias_ref[...] = jnp.broadcast_to(
                    jnp.sum(turned, axis=1, keepdims=True), bias_ref.shape
                )
            else:
                at = (k if k == 0 else k - 1) * 384
                coef_ref[:, at : at + 384] = turned.astype(BF16)

    for lat in range(LDEV):
        wait_space(back_rows, got_rows, recv_sem, 1, lat)
        rows[lat] = got_rows[lat].astype(F32)
        for row in range(MAIN):
            flat[pl.ds(row, 64, stride=SLOTS), :] = rows[lat, pl.ds(row, 64, stride=16), :]
        for i in range(SLOTS - MAIN):
            thirds = [
                pltpu.roll(
                    rows[lat, pl.ds(3 * i + th, 64, stride=16), :], (32 + 32 * th) % 128, 1
                )
                for th in range(3)
            ]
            flat[pl.ds(MAIN + i, 64, stride=SLOTS), :] = jnp.where(
                lane < 32, thirds[0], jnp.where(lane < 64, thirds[1], thirds[2])
            )
        for start in range(0, COLS, 128):
            gathered[:, start : start + 128] = (
                flat[start : start + 128, :].T[0:96].astype(BF16)
            )
        total = lax.dot_general(
            gathered[...], hot[...], (((1,), (1,)), ((), ())), preferred_element_type=F32
        )
        for k in range(2):
            modes[:, k * MPAD : (k + 1) * MPAD] = total[k * CDEV : k * CDEV + CDEV].astype(BF16)
        for strip in range(6):
            spatial = jnp.dot(
                modes[...],
                inverse_ref[:, strip * 256 : strip * 256 + 256],
                preferred_element_type=F32,
            )
            for block in (2 * strip, 2 * strip + 1):
                lanes = slice(block * 128, block * 128 + 128)
                if block < 11:
                    old = x_ref[lat, :, lanes].astype(F32)
                else:
                    old = jnp.concatenate(
                        [x_ref[lat, :, 1408:1440], jnp.zeros((CDEV, 96), BF16)], axis=1
                    ).astype(F32)
                at = (block % 2) * 128
                new = (old + spatial[:, at : at + 128]).astype(BF16)
                for part, place in places(lat, block):
                    updated[lat, part, :, place * 128 : place * 128 + 128] = new
        send_chan(updated, whole, 0, lat)
        if lat == 0:
            prepare_coef()
        else:
            mix(lat - 1)
    mix(LDEV - 1)
    for lat in range(LDEV):
        wait_chan(mixed, final, chan_recv, 1, lat)
        wait_space(out_rows, in_rows, send_sem, 0, lat)
        wait_space(back_rows, got_rows, send_sem, 1, lat)
        wait_chan(updated, whole, chan_send, 0, lat)
        wait_chan(mixed, final, chan_send, 1, lat)
    wait_coef(3, coef_send.at[0])
    wait_coef(4, coef_send.at[1])


def unpack_kernel(final_ref, out_ref):
    for lat in range(LDEV):
        for block in range(12):
            part, place = places(lat, block)[0]
            width = 128 if block < 11 else 32
            out_ref[lat, :, block * 128 : block * 128 + width] = final_ref[
                lat, part, :, place * 128 : place * 128 + width
            ]


def shards(state_field, slot_wave, spectral_filter, kan_coef):
    forward, inverse, weights, xrow, first, steps = make_tables()
    x = jnp.transpose(state_field, (1, 0, 2))
    cols = slot_wave.reshape(1, COLS)
    message = pltpu.VMEM((LDEV, SPACES * 16, 128), BF16)
    part = pltpu.VMEM((LDEV, CHANS, CDEV, PART), BF16)
    final = pl.pallas_call(
        block_kernel,
        out_shape=jax.ShapeDtypeStruct((LDEV, CHANS, CDEV, PART), BF16),
        in_specs=[HBM] * 5 + [SMEM] * 3 + [VMEM] * 3,
        out_specs=VMEM,
        scratch_shapes=[
            pltpu.VMEM((LDEV, CDEV, NLON), BF16),
            pltpu.VMEM((2, NLON, MPAD), BF16),
            pltpu.VMEM((2 * MPAD, NPAD), BF16),
            pltpu.VMEM((SLOTS, 2, CDEV, LMAX), BF16),
            pltpu.VMEM((2, CHANS // 2, BASIS, CDEV, 384), BF16),
            pltpu.SemaphoreType.DMA((6,)),
            pltpu.SemaphoreType.DMA((2, LDEV)),
            pltpu.SemaphoreType.DMA((2, LDEV)),
            pltpu.SemaphoreType.DMA((2, LDEV)),
            pltpu.SemaphoreType.DMA((2, LDEV)),
            pltpu.SemaphoreType.DMA((2,)),
            pltpu.SemaphoreType.DMA((2,)),
            pltpu.VMEM((MPAD, COLS), BF16),
            pltpu.VMEM((96, MPAD), BF16),
            pltpu.VMEM((96, COLS), F32),
            pltpu.VMEM((COLS, 128), F32),
            pltpu.VMEM((LDEV, SPACES * 16, 128), F32),
            message,
            message,
            pltpu.VMEM((DEG_SLOTS, 128), jnp.int32),
            pltpu.VMEM((DEG_SLOTS, 256), F32),
            pltpu.VMEM((2, CHUNK * DEG_SLOTS, 128), F32),
            pltpu.VMEM((SLOTS, LMAX, 256), BF16),
            pltpu.VMEM((SLOTS, 96, 256), BF16),
            pltpu.VMEM((SLOTS, 96, 256), F32),
            message,
            message,
            pltpu.VMEM((384, 5 * 384), BF16),
            pltpu.VMEM((384, 128), F32),
            pltpu.VMEM((96, COLS), BF16),
            pltpu.VMEM((CDEV, 2 * MPAD), BF16),
            pltpu.VMEM((5 * 384, PART), BF16),
            part,
            part,
            part,
        ],
        compiler_params=pltpu.CompilerParams(
            collective_id=0, has_side_effects=True, vmem_limit_bytes=60 * 1024 * 1024
        ),
        name="spectral_block",
    )(x, forward, inverse, spectral_filter, kan_coef, slot_wave, weights, steps, cols, xrow, first)
    out = pl.pallas_call(
        unpack_kernel,
        out_shape=jax.ShapeDtypeStruct((LDEV, CDEV, NLON), BF16),
        in_specs=[VMEM],
        out_specs=VMEM,
        name="unpack",
    )(final)
    return jnp.transpose(out, (1, 0, 2))


def solution(mesh):
    in_specs = (
        P("chan", "space", None),
        P(),
        P("space", None, "chan", None),
        P(None, "chan", None),
    )
    out_specs = P("chan", "space", None)
    return jax.shard_map(shards, mesh=mesh, in_specs=in_specs, out_specs=out_specs, check_vma=False)
```
